32 devices in a mesh: seq: 8 (over z, y), head: 4 (over x, core).
Axes of the slice: x: 2, y: 2, z: 4, core: 2. Of those that a mesh axis runs over, the one named last changes fastest.
Arguments:
- tokens: bfloat16 [8192, 2048], P('seq'), may hold values from -6 to 6
- cotangent: bfloat16 [8192, 2048], P('seq'), may hold values from -6 to 6
- prefix_length: int32 [1], replicated, may hold values from 1793 to 2048
- answer_lengths: int32 [8], P('seq'), may hold values from 1 to 768, as said below
- inward: float32 [2048, 3, 2048], P('seq', None, 'head'), may hold values from -0.125 to 0.125
- outward: float32 [2048, 2048], P('head', 'seq'), may hold values from -1.75 to 1.75
- expand: float32 [2048, 8192], P('seq', 'head')
- contract: float32 [8192, 2048], P('head', 'seq'), may hold values from -0.0625 to 0.0625
- norm_gains: float32 [2, 2048], P(None, 'seq')
- moment_inward: float32 [2048, 3, 2048], P('seq', None, 'head'), may hold values from -9.1552734e-05 to 9.1552734e-05
- moment_outward: float32 [2048, 2048], P('head', 'seq'), may hold values from -9.1552734e-05 to 9.1552734e-05
- moment_expand: float32 [2048, 8192], P('seq', 'head'), may hold values from -9.1552734e-05 to 9.1552734e-05
- moment_contract: float32 [8192, 2048], P('head', 'seq'), may hold values from -9.1552734e-05 to 9.1552734e-05
- moment_gains: float32 [2, 2048], P(None, 'seq'), may hold values from -0.00036621094 to 0.00036621094
- variance_inward: float32 [2048, 3, 2048], P('seq', None, 'head'), may hold values from 5.9604643e-10 to 7.947286e-09
- variance_outward: float32 [2048, 2048], P('head', 'seq'), may hold values from 1.622759e-11 to 2.187197e-10
- variance_expand: float32 [2048, 8192], P('seq', 'head'), may hold values from 9.934108e-11 to 1.390775e-09
- variance_contract: float32 [8192, 2048], P('head', 'seq'), may hold values from 5.9604643e-10 to 7.947286e-09
- variance_gains: float32 [2, 2048], P(None, 'seq'), may hold values from 9.536743e-09 to 1.2715658e-07
- average_inward: float32 [2048, 3, 2048], P('seq', None, 'head'), may hold values from -0.125 to 0.125
- average_outward: float32 [2048, 2048], P('head', 'seq'), may hold values from -1.75 to 1.75
- average_expand: float32 [2048, 8192], P('seq', 'head'), may hold values from -0.125 to 0.125
- average_contract: float32 [8192, 2048], P('head', 'seq'), may hold values from -0.0625 to 0.0625
- average_gains: float32 [2, 2048], P(None, 'seq'), may hold values from 0.5 to 1.5
Outputs:
- layer_output: bfloat16 [8192, 2048], P('seq')
- input_grad: float32 [8192, 2048], P('seq')
- grad_norm: float32 [1], replicated
- inward_moment: float32 [2048, 3, 2048], P('seq', None, 'head')
- inward_variance: float32 [2048, 3, 2048], P('seq', None, 'head')
- inward_weight: float32 [2048, 3, 2048], P('seq', None, 'head')
- inward_average: float32 [2048, 3, 2048], P('seq', None, 'head')
- outward_moment: float32 [2048, 2048], P('head', 'seq')
- outward_variance: float32 [2048, 2048], P('head', 'seq')
- outward_weight: float32 [2048, 2048], P('head', 'seq')
- outward_average: float32 [2048, 2048], P('head', 'seq')
- expand_moment: float32 [2048, 8192], P('seq', 'head')
- expand_variance: float32 [2048, 8192], P('seq', 'head')
- expand_weight: float32 [2048, 8192], P('seq', 'head')
- expand_average: float32 [2048, 8192], P('seq', 'head')
- contract_moment: float32 [8192, 2048], P('head', 'seq')
- contract_variance: float32 [8192, 2048], P('head', 'seq')
- contract_weight: float32 [8192, 2048], P('head', 'seq')
- contract_average: float32 [8192, 2048], P('head', 'seq')
- gains_moment: float32 [2, 2048], P(None, 'seq')
- gains_variance: float32 [2, 2048], P(None, 'seq')
- gains_weight: float32 [2, 2048], P(None, 'seq')
- gains_average: float32 [2, 2048], P(None, 'seq')
The draws below stay inside these ranges and needn't reach their ends.
Inputs may be any that keep to these rules, and one draw needn't show every extreme that they name: Prefix slots at positions from prefix_length on are padding. Solution slots from answer_lengths[i] on are padding; some solution fills all 768 slots in every draw.
All inputs are finite; a program needn't handle non-finite values.
Results may differ from the reference program's by a relative error of at most 0.024.
Values may be sent and summed in bfloat16 or wider, within the bound.
No kernel may reach another device: no remote copies, remote signals or barrier semaphores. Data moves between devices by JAX's collectives and lax.ppermute only.
A program may use at most 320 MiB of HBM per device.

```python
import math
import jax
import jax.numpy as jnp
from jax import lax

D = 2048
HEADS = 16
HEAD_DIM = 128
FF = 8192
PRE_DEV = 256
SOL_DEV = 768
STEP = 10
PREFIX = 2048
TOKENS = 8192
N_SEQ = 8


def draw_answer_lengths(key, part):
    key = jax.random.fold_in(key, 11)
    device_order = jnp.arange(N_SEQ, dtype=jnp.int32)
    base_length = SOL_DEV // 8 + (SOL_DEV - SOL_DEV // 8) * (device_order + 1) // N_SEQ
    jitter = jax.random.randint(key, (N_SEQ,), 0, SOL_DEV // 8 + 1, dtype=jnp.int32)
    lengths = jnp.maximum(base_length - jitter, 1)
    return jnp.where(device_order == N_SEQ - 1, SOL_DEV, lengths).astype(jnp.int32)


def draw_norm_gains(key, part):
    key = jax.random.fold_in(key, 5)
    position = jnp.arange(D, dtype=jnp.float32) / D
    column_scale = 0.6 * jnp.exp(position * math.log(3.0))
    jitter_factor = jax.random.uniform(key, (2, D), jnp.float32, 0.7, 1.4)
    return (column_scale[None] * jitter_factor).astype(jnp.float32)


def draw_expand(key, part):
    key = jax.random.fold_in(key, 7)
    position = jnp.arange(FF, dtype=jnp.float32) / FF
    column_scale = 0.6 * jnp.exp(position * math.log(3.0))
    entries = jax.random.normal(key, (D, FF), jnp.float32)
    return (entries * column_scale[None] * D ** (-0.5)).astype(jnp.float32)


def levels(rng, shape, shards, low, largest):
    loudness, own = 1.0, jax.random.fold_in(rng, 6)
    for axis_at, shards_of in shards:
        heights = jnp.exp(jax.random.uniform(jax.random.fold_in(own, axis_at), (shards_of,), jnp.float32, low / len(shards), largest / len(shards)))
        loudness = loudness * jnp.repeat(heights, shape[axis_at] // shards_of).reshape([-1 if axis == axis_at else 1 for axis in range(len(shape))])
    return loudness


def scatter_about(stream_key, shape, scale, most, shards=(), held_as=jnp.bfloat16):
    values = scale * jax.random.normal(stream_key, shape, jnp.float32)
    if shards:
        values = values * levels(stream_key, shape, shards, -0.22, 0.18)
    return jnp.clip(values, -most, most).astype(held_as)


def setup_inputs(seed: int = 0) -> dict:
    key_of = jax.random.split(jax.random.key(seed), 25)
    return {
        "tokens": scatter_about(key_of[0], (TOKENS, D), 1.0, 6.0, ((0, 8),)),
        "cotangent": scatter_about(key_of[1], (TOKENS, D), 1.0, 6.0, ((0, 8),)),
        "prefix_length": jax.random.randint(key_of[2], (1,), PREFIX - PRE_DEV + 1, PREFIX + 1).astype(jnp.int32),
        "answer_lengths": draw_answer_lengths(jax.random.fold_in(key_of[24], 71), 0),
        "inward": scatter_about(key_of[4], (D, 3, D), D ** -0.5, 0.125, ((0, 8), (2, 4)), jnp.float32),
        "outward": scatter_about(key_of[5], (D, D), (max(D * 16 // (PRE_DEV * N_SEQ + SOL_DEV), 1)) ** -0.5, 1.75, ((0, 4), (1, 8)), jnp.float32),
        "expand": draw_expand(jax.random.fold_in(key_of[24], 71), 0),
        "contract": scatter_about(key_of[7], (FF, D), FF ** -0.5, 0.0625, ((0, 4), (1, 8)), jnp.float32),
        "norm_gains": draw_norm_gains(jax.random.fold_in(key_of[24], 71), 0),
        "moment_inward": scatter_about(key_of[9], (D, 3, D), (0.11 * (4 * D * D + 2 * D * FF) ** -0.5), 9.1552734375e-05, ((0, 8), (2, 4)), jnp.float32),
        "moment_outward": scatter_about(key_of[10], (D, D), (0.11 * (4 * D * D + 2 * D * FF) ** -0.5), 9.1552734375e-05, ((0, 4), (1, 8)), jnp.float32),
        "moment_expand": scatter_about(key_of[11], (D, FF), (0.11 * (4 * D * D + 2 * D * FF) ** -0.5), 9.1552734375e-05, ((0, 8), (1, 4)), jnp.float32),
        "moment_contract": scatter_about(key_of[12], (FF, D), (0.11 * (4 * D * D + 2 * D * FF) ** -0.5), 9.1552734375e-05, ((0, 4), (1, 8)), jnp.float32),
        "moment_gains": scatter_about(key_of[13], (2, D), (0.44 * (4 * D * D + 2 * D * FF) ** -0.5), 0.00036621094, ((1, 8),), jnp.float32),
        "variance_inward": jnp.clip(jnp.exp(math.log(7.947286384535346e-09) - 2.5902672 * jax.random.uniform(key_of[14], (D, 3, D), jnp.float32) ** levels(key_of[14], (D, 3, D), ((0, 8), (2, 4)), -0.2, 0.2)), 5.9604643443123e-10, 7.947286384535346e-09),
        "variance_outward": jnp.clip(jnp.exp(math.log(2.1871969513309608e-10) - 2.601078 * jax.random.uniform(key_of[15], (D, D), jnp.float32) ** levels(key_of[15], (D, D), ((0, 4), (1, 8)), -0.2, 0.2)), 1.6227590451944884e-11, 2.1871969513309608e-10),
        "variance_expand": jnp.clip(jnp.exp(math.log(1.390775050680304e-09) - 2.6390573 * jax.random.uniform(key_of[16], (D, FF), jnp.float32) ** levels(key_of[16], (D, FF), ((0, 8), (1, 4)), -0.2, 0.2)), 9.934107703113426e-11, 1.390775050680304e-09),
        "variance_contract": jnp.clip(jnp.exp(math.log(7.947286384535346e-09) - 2.5902672 * jax.random.uniform(key_of[17], (FF, D), jnp.float32) ** levels(key_of[17], (FF, D), ((0, 4), (1, 8)), -0.2, 0.2)), 5.9604643443123e-10, 7.947286384535346e-09),
        "variance_gains": jnp.clip(jnp.exp(math.log(1.2715658215256553e-07) - 2.5902672 * jax.random.uniform(key_of[18], (2, D), jnp.float32) ** levels(key_of[18], (2, D), ((1, 8),), -0.2, 0.2)), 9.53674295089968e-09, 1.2715658215256553e-07),
        "average_inward": scatter_about(key_of[19], (D, 3, D), D ** -0.5, 0.125, ((0, 8), (2, 4)), jnp.float32),
        "average_outward": scatter_about(key_of[20], (D, D), (max(D * 16 // (PRE_DEV * N_SEQ + SOL_DEV), 1)) ** -0.5, 1.75, ((0, 4), (1, 8)), jnp.float32),
        "average_expand": scatter_about(key_of[21], (D, FF), D ** -0.5, 0.125, ((0, 8), (1, 4)), jnp.float32),
        "average_contract": scatter_about(key_of[22], (FF, D), FF ** -0.5, 0.0625, ((0, 4), (1, 8)), jnp.float32),
        "average_gains": jnp.clip(1.0 + 0.1 * jax.random.normal(key_of[23], (2, D), jnp.float32), 0.5, 1.5),
    }


EPS_NORM = 1e-05
BETA_ONE = 0.9
BETA_TWO = 0.95
ADAM_EPS = 1e-08
EMA_KEEP = 0.7
CLIP_NORM = 1.0
DECAY_MATRIX = 0.1
RATE_INWARD = 0.05
RATE_OUTWARD = 0.15
RATE_EXPAND = 0.05
RATE_CONTRACT = 0.03
RATE_GAINS = 0.5
HIGHEST_PRECISION = lax.Precision.HIGHEST

@jax.custom_vjp
def low(v):
    return lax.optimization_barrier(v.astype(jnp.bfloat16)).astype(jnp.float32)

@jax.custom_vjp
def low_back(v):
    return v

def low_keep(v):
    return (low(v), None)

def low_pass(kept, grad):
    return (grad,)

def back_keep(v):
    return (v, None)

def back_low(kept, grad):
    return (low(grad),)
low.defvjp(low_keep, low_pass)
low_back.defvjp(back_keep, back_low)

def layer_norm(values, gain_row):
    center = values - lax.optimization_barrier(jnp.mean(values, axis=-1, keepdims=True))
    spread = lax.optimization_barrier(jnp.mean(center * center, axis=-1, keepdims=True))
    return center * lax.rsqrt(spread + EPS_NORM) * gain_row

def attend(queries, key_rows, value_rows, allowed):
    score_scale = queries.shape[-1] ** (-0.5)
    scores = low_back(jnp.einsum('qhd,khd->hqk', queries, key_rows, precision=HIGHEST_PRECISION) * score_scale)
    scores = jnp.where(allowed[None], scores, -1e+30)
    probabilities = low(jax.nn.softmax(scores, axis=-1))
    return jnp.einsum('hqk,khd->qhd', probabilities, value_rows, precision=HIGHEST_PRECISION)

def forward(tokens, inward, outward, expand, contract, norm_gains, prefix_length, answer_lengths):
    gain_pair = low(norm_gains)
    normed_one = low(layer_norm(tokens, gain_pair[0]))
    projected = jnp.einsum('td,dcn->tcn', normed_one, low(inward), precision=HIGHEST_PRECISION)
    projected = low_back(low(projected))
    head_split = projected.reshape(N_SEQ, PRE_DEV + SOL_DEV, 3, HEADS, HEAD_DIM)
    prefix = head_split[:, :PRE_DEV].reshape(PREFIX, 3, HEADS, HEAD_DIM)
    answer = head_split[:, PRE_DEV:]
    prefix_spot = jnp.arange(PREFIX)

    def prefix_block(inputs_pair):
        query_rows, shard_index = inputs_pair
        position = shard_index * PRE_DEV + jnp.arange(PRE_DEV)
        allowed = (prefix_spot[None] <= position[:, None]) & (prefix_spot[None] < prefix_length[0])
        return attend(query_rows, prefix[:, 1], prefix[:, 2], allowed)
    prefix_out = lax.map(jax.checkpoint(prefix_block), (prefix[:, 0].reshape(N_SEQ, PRE_DEV, HEADS, HEAD_DIM), jnp.arange(N_SEQ)))
    column = jnp.arange(PREFIX + SOL_DEV)
    answer_spot = jnp.arange(SOL_DEV)

    def answer_block(inputs_pair):
        answer_rows, answer_limit = inputs_pair
        key_rows = jnp.concatenate([prefix[:, 1], answer_rows[:, 1]], axis=0)
        value_rows = jnp.concatenate([prefix[:, 2], answer_rows[:, 2]], axis=0)
        allowed = jnp.where(column[None] < PREFIX, column[None] < prefix_length[0], (column[None] - PREFIX <= answer_spot[:, None]) & (column[None] - PREFIX < answer_limit))
        return attend(answer_rows[:, 0], key_rows, value_rows, allowed)
    answer_out = lax.map(jax.checkpoint(answer_block), (answer, answer_lengths))
    mixed_heads = jnp.concatenate([prefix_out, answer_out], axis=1).reshape(N_SEQ * (PRE_DEV + SOL_DEV), HEADS * HEAD_DIM)
    mixed_heads = low_back(low(mixed_heads))
    attention = low_back(jnp.dot(mixed_heads, low(outward), precision=HIGHEST_PRECISION))
    hidden = tokens + attention
    normed_two = low(layer_norm(hidden, gain_pair[1]))
    up_values = low_back(jnp.dot(normed_two, low(expand), precision=HIGHEST_PRECISION))
    activation = low(jax.nn.gelu(up_values, approximate=True))
    return hidden + jnp.dot(activation, low(contract), precision=HIGHEST_PRECISION)

def adamw(weight, gradient, moment, variance, average, step_rate, decay_rate):
    moment = BETA_ONE * moment + (1.0 - BETA_ONE) * gradient
    variance = BETA_TWO * variance + (1.0 - BETA_TWO) * gradient * gradient
    corrected = moment / (1.0 - BETA_ONE ** STEP)
    scaled_root = jnp.sqrt(variance / (1.0 - BETA_TWO ** STEP)) + ADAM_EPS
    weight_new = weight - step_rate * corrected / scaled_root - step_rate * decay_rate * weight
    average = EMA_KEEP * average + (1.0 - EMA_KEEP) * weight_new
    return (moment, variance, weight_new, average)

def reference(tokens, cotangent, prefix_length, answer_lengths, inward, outward, expand, contract, norm_gains, moment_inward, moment_outward, moment_expand, moment_contract, moment_gains, variance_inward, variance_outward, variance_expand, variance_contract, variance_gains, average_inward, average_outward, average_expand, average_contract, average_gains):
    prefix_rows = jnp.arange(N_SEQ)[:, None] * PRE_DEV + jnp.arange(PRE_DEV)[None]
    prefix_live = prefix_rows < prefix_length[0]
    answer_live = jnp.arange(SOL_DEV)[None] < answer_lengths[:, None]
    valid_rows = jnp.concatenate([prefix_live, answer_live], axis=1).reshape(-1, 1).astype(jnp.float32)

    def closed(source, first_matrix, second_matrix, third_matrix, fourth_matrix, gain_matrix):
        return forward(source, first_matrix, second_matrix, third_matrix, fourth_matrix, gain_matrix, prefix_length, answer_lengths)
    result, pullback = jax.vjp(closed, tokens.astype(jnp.float32), inward, outward, expand, contract, norm_gains)
    gradients = pullback(cotangent.astype(jnp.float32) * valid_rows)
    squares = jnp.float32(0.0)
    for gradient in gradients[1:]:
        squares = squares + jnp.sum(gradient * gradient)
    grad_norm = jnp.sqrt(squares)
    factor = CLIP_NORM / jnp.maximum(grad_norm, CLIP_NORM)
    in_new = adamw(inward, gradients[1] * factor, moment_inward, variance_inward, average_inward, RATE_INWARD, DECAY_MATRIX)
    out_new = adamw(outward, gradients[2] * factor, moment_outward, variance_outward, average_outward, RATE_OUTWARD, DECAY_MATRIX)
    up_new = adamw(expand, gradients[3] * factor, moment_expand, variance_expand, average_expand, RATE_EXPAND, DECAY_MATRIX)
    down_new = adamw(contract, gradients[4] * factor, moment_contract, variance_contract, average_contract, RATE_CONTRACT, DECAY_MATRIX)
    gain_new = adamw(norm_gains, gradients[5] * factor, moment_gains, variance_gains, average_gains, RATE_GAINS, 0.0)
    return (result.astype(jnp.bfloat16), gradients[0], grad_norm.reshape(1), in_new[0], in_new[1], in_new[2], in_new[3], out_new[0], out_new[1], out_new[2], out_new[3], up_new[0], up_new[1], up_new[2], up_new[3], down_new[0], down_new[1], down_new[2], down_new[3], gain_new[0], gain_new[1], gain_new[2], gain_new[3])
```

```python
import functools

import jax
import jax.numpy as jnp
from jax import lax
from jax.experimental import pallas as pl
from jax.experimental.pallas import tpu as pltpu
from jax.sharding import PartitionSpec as P

HEAD_DIM = 128
PRE_DEV = 256
SOL_DEV = 768
STEP = 10
BLOCK = 256

EPS_NORM = 1e-05
BETA_ONE = 0.9
BETA_TWO = 0.95
ADAM_EPS = 1e-08
EMA_KEEP = 0.7
CLIP_NORM = 1.0
DECAY_MATRIX = 0.1
RATE_INWARD = 0.05
RATE_OUTWARD = 0.15
RATE_EXPAND = 0.05
RATE_CONTRACT = 0.03
RATE_GAINS = 0.5

LOG2E = 1.4426950408889634
MASKED = -1e30
BF = jnp.bfloat16
FP = jnp.float32
VMEM_LIMIT = 56 * 1024 * 1024


def ring_order(count):
    depth = 4
    if count % depth or (count // depth) % 2:
        return list(range(count))
    width = count // depth
    order = [z * width for z in range(depth)]
    across = list(range(1, width))
    for z in reversed(range(depth)):
        order += [z * width + y for y in across]
        across = across[::-1]
    return order


class Ring:
    def __init__(self, count):
        self.count = count
        self.half = count // 2
        self.order = ring_order(count)
        self.up = [(self.order[i], self.order[(i + 1) % count]) for i in range(count)]
        self.down = [(b, a) for a, b in self.up]
        inverse = [0] * count
        for i, s in enumerate(self.order):
            inverse[s] = i
        self.inverse = inverse

    def ids(self):
        place = jnp.asarray(self.inverse, jnp.int32)[lax.axis_index("seq")]
        spots = (place + jnp.arange(self.count, dtype=jnp.int32)) % self.count
        return jnp.asarray(self.order, jnp.int32)[spots]

    def blocks_of(self):
        place = jnp.asarray(self.inverse, jnp.int32)[lax.axis_index("seq")]
        return (jnp.asarray(self.inverse, jnp.int32) - place) % self.count

    def gather(self, own):
        n, half = self.count, self.half
        blocks = [None] * n
        blocks[0] = own
        from_up = from_down = own
        for j in range(1, half):
            from_up = lax.ppermute(from_up, "seq", self.down)
            from_down = lax.ppermute(from_down, "seq", self.up)
            blocks[j] = from_up
            blocks[n - j] = from_down
        mid = own.shape[0] // 2
        blocks[half] = jnp.concatenate(
            [
                lax.ppermute(from_up[:mid], "seq", self.down),
                lax.ppermute(from_down[mid:], "seq", self.up),
            ],
            axis=0,
        )
        return blocks

    def scatter_sum(self, part):
        n, half = self.count, self.half
        far = part(half)
        mid = far.shape[0] // 2
        rising = lax.ppermute(far[:mid].astype(BF), "seq", self.up)
        falling = lax.ppermute(far[mid:].astype(BF), "seq", self.down)
        for j in range(half - 1, 0, -1):
            up_term = part(j)
            down_term = part(n - j)
            if j == half - 1:
                up_sum = jnp.concatenate([up_term[:mid] + rising.astype(FP), up_term[mid:]], 0)
                down_sum = jnp.concatenate([down_term[:mid], down_term[mid:] + falling.astype(FP)], 0)
            else:
                up_sum = up_term + rising.astype(FP)
                down_sum = down_term + falling.astype(FP)
            rising = lax.ppermute(up_sum.astype(BF), "seq", self.up)
            falling = lax.ppermute(down_sum.astype(BF), "seq", self.down)
        return part(0) + rising.astype(FP) + falling.astype(FP)


class Team:
    def __init__(self, count, rows):
        self.cores = 2 if count % 2 == 0 else 1
        self.chips = count // self.cores
        self.count = count
        self.half = rows // self.cores
        self.quarter = self.half // self.chips
        self.core_flip = [(i, i ^ 1) for i in range(count)]

    def shift(self, k):
        chips, cores = self.chips, self.cores
        return [
            (x * cores + c, ((x + k) % chips) * cores + c) for x in range(chips) for c in range(cores)
        ]

    def place(self):
        index = lax.axis_index("head")
        return index // self.cores, index % self.cores

    def first_row(self):
        x, c = self.place()
        return c * self.half + x * self.quarter

    def scatter_sum(self, part):
        x, c = self.place()
        got = None
        if self.cores == 2:
            away = part((1 - c) * self.half, self.half).astype(BF)
            got = lax.ppermute(away, "head", self.core_flip)

        def chip_sum(spot):
            term = part(c * self.half + spot * self.quarter, self.quarter)
            if got is None:
                return term
            other = lax.dynamic_slice_in_dim(got, spot * self.quarter, self.quarter, 0)
            return term + other.astype(FP)

        arrived = []
        for k in range(1, self.chips):
            arrived.append(
                lax.ppermute(chip_sum((x + k) % self.chips).astype(BF), "head", self.shift(k))
            )
        total = chip_sum(x)
        for other in arrived:
            total = total + other.astype(FP)
        return total

    def gather(self, own):
        x, c = self.place()
        parts = [own] + [lax.ppermute(own, "head", self.shift(-k)) for k in range(1, self.chips)]
        ordered = []
        for spot in range(self.chips):
            piece = parts[0]
            for k in range(1, self.chips):
                piece = jnp.where((spot - x) % self.chips == k, parts[k], piece)
            ordered.append(piece)
        half = jnp.concatenate(ordered, axis=0) if self.chips > 1 else own
        if self.cores == 1:
            return half
        other = lax.ppermute(half, "head", self.core_flip)
        return jnp.concatenate([jnp.where(c == 0, half, other), jnp.where(c == 0, other, half)], axis=0)


def total_of_all(value, seq_count, head_count):
    for axis, count in (("head", head_count), ("seq", seq_count)):
        step = 1
        while step < count:
            value = value + lax.ppermute(value, axis, [(i, i ^ step) for i in range(count)])
            step *= 2
    return value


def pick_columns(array, ids):
    rows, width = array.shape
    count = ids.shape[0]
    size = width // count

    def body(ids_ref, in_ref, out_ref):
        out_ref[...] = in_ref[...]

    return pl.pallas_call(
        body,
        grid_spec=pltpu.PrefetchScalarGridSpec(
            num_scalar_prefetch=1,
            grid=(count,),
            in_specs=[pl.BlockSpec((rows, size), lambda b, ids_ref: (0, ids_ref[b]))],
            out_specs=pl.BlockSpec((rows, size), lambda b, ids_ref: (0, b)),
        ),
        out_shape=jax.ShapeDtypeStruct(array.shape, array.dtype),
        compiler_params=pltpu.CompilerParams(vmem_limit_bytes=VMEM_LIMIT),
        name="pick_columns",
    )(ids, array)


def dot_nt(a, b):
    return lax.dot_general(a, b, (((1,), (1,)), ((), ())), preferred_element_type=FP)


def dot_nn(a, b):
    return lax.dot_general(a, b, (((1,), (0,)), ((), ())), preferred_element_type=FP)


def dot_tn(a, b):
    return lax.dot_general(a, b, (((0,), (0,)), ((), ())), preferred_element_type=FP)


def prefix_places(meta_ref, n):
    spot = lax.broadcasted_iota(jnp.int32, (1, PRE_DEV), 1)
    return jnp.concatenate([spot + meta_ref[3 + b] * PRE_DEV for b in range(n)], axis=1)


def masked_scores(meta_ref, q_ref, k_ref, kp_ref, places, block):
    limit_prefix = meta_ref[1]
    limit_answer = meta_ref[2]
    query = q_ref[pl.ds(block * BLOCK, BLOCK), :]
    score_pre = dot_nt(query, kp_ref[0])
    if block < PRE_DEV // BLOCK:
        row = lax.broadcasted_iota(jnp.int32, (BLOCK, 1), 0) + block * BLOCK
        reach = jnp.minimum(meta_ref[0] * PRE_DEV + row + 1, limit_prefix)
        return query, jnp.where(places < reach, score_pre, MASKED), None
    score_pre = jnp.where(places < limit_prefix, score_pre, MASKED)
    solution_row = block * BLOCK - PRE_DEV
    width = solution_row + BLOCK
    score_own = dot_nt(query, k_ref[pl.ds(PRE_DEV, width), :])
    row = lax.broadcasted_iota(jnp.int32, (BLOCK, 1), 0) + solution_row
    reach = jnp.minimum(row + 1, limit_answer)
    column = lax.broadcasted_iota(jnp.int32, (1, width), 1)
    return query, score_pre, jnp.where(column < reach, score_own, MASKED)


def attention_forward(meta, projected, prefix_kv):
    rows, width3 = projected.shape
    heads = width3 // (3 * HEAD_DIM)
    prefix = prefix_kv.shape[1]
    n = prefix // PRE_DEV
    scale = HEAD_DIM ** (-0.5) * LOG2E

    def body(meta_ref, q_ref, k_ref, v_ref, kp_ref, vp_ref, out_ref, log_ref):
        places = prefix_places(meta_ref, n)
        for block in range(rows // BLOCK):
            _, score_pre, score_own = masked_scores(meta_ref, q_ref, k_ref, kp_ref, places, block)
            top = jnp.max(score_pre, axis=-1, keepdims=True)
            if score_own is not None:
                top = jnp.maximum(top, jnp.max(score_own, axis=-1, keepdims=True))
            e_pre = jnp.exp2((score_pre - top) * scale)
            total = jnp.sum(e_pre, axis=-1, keepdims=True)
            out = dot_nn(e_pre.astype(BF), vp_ref[0])
            if score_own is not None:
                e_own = jnp.exp2((score_own - top) * scale)
                total = total + jnp.sum(e_own, axis=-1, keepdims=True)
                out = out + dot_nn(e_own.astype(BF), v_ref[pl.ds(PRE_DEV, score_own.shape[1]), :])
            out_ref[pl.ds(block * BLOCK, BLOCK), :] = (out / total).astype(BF)
            log_ref[0, pl.ds(block * BLOCK, BLOCK), :] = top * scale + jnp.log2(total)

    spec = lambda shift: pl.BlockSpec((rows, HEAD_DIM), lambda h, m: (0, h + shift))
    pre = lambda which: pl.BlockSpec((1, prefix, HEAD_DIM), lambda h, m: (which, 0, h))
    return pl.pallas_call(
        body,
        grid_spec=pltpu.PrefetchScalarGridSpec(
            num_scalar_prefetch=1,
            grid=(heads,),
            in_specs=[spec(0), spec(heads), spec(2 * heads), pre(0), pre(1)],
            out_specs=[spec(0), pl.BlockSpec((1, rows, 1), lambda h, m: (h, 0, 0))],
        ),
        out_shape=[
            jax.ShapeDtypeStruct((rows, heads * HEAD_DIM), BF),
            jax.ShapeDtypeStruct((heads, rows, 1), FP),
        ],
        compiler_params=pltpu.CompilerParams(vmem_limit_bytes=VMEM_LIMIT),
        name="attention_forward",
    )(meta, projected, projected, projected, prefix_kv, prefix_kv)


def attention_backward(meta, projected, prefix_kv, mixed, d_mixed, logs):
    rows, width3 = projected.shape
    heads = width3 // (3 * HEAD_DIM)
    prefix = prefix_kv.shape[1]
    n = prefix // PRE_DEV
    scale = HEAD_DIM ** (-0.5)

    def body(
        meta_ref, q_ref, k_ref, v_ref, kp_ref, vp_ref, o_ref, do_ref, log_ref,
        dq_ref, dpre_ref, dsol_ref, dk_pre, dv_pre, dk_own, dv_own,
    ):
        places = prefix_places(meta_ref, n)
        dk_own[...] = jnp.zeros_like(dk_own)
        dv_own[...] = jnp.zeros_like(dv_own)
        for block in range(rows // BLOCK):
            spot = pl.ds(block * BLOCK, BLOCK)
            query, score_pre, score_own = masked_scores(
                meta_ref, q_ref, k_ref, kp_ref, places, block
            )
            d_out = do_ref[spot, :]
            log = log_ref[0, spot, :]
            inner = jnp.sum(d_out.astype(FP) * o_ref[spot, :].astype(FP), axis=-1, keepdims=True)
            p = jnp.exp2(score_pre * (scale * LOG2E) - log)
            ds = (p * (dot_nt(d_out, vp_ref[0]) - inner)).astype(BF)
            p = p.astype(BF)
            dq = dot_nn(ds, kp_ref[0])
            dk_term = dot_tn(ds, query)
            dv_term = dot_tn(p, d_out)
            if block == 0:
                dk_pre[...] = dk_term
                dv_pre[...] = dv_term
            else:
                dk_pre[...] += dk_term
                dv_pre[...] += dv_term
            if score_own is not None:
                keys = pl.ds(PRE_DEV, score_own.shape[1])
                p = jnp.exp2(score_own * (scale * LOG2E) - log)
                ds = (p * (dot_nt(d_out, v_ref[keys, :]) - inner)).astype(BF)
                p = p.astype(BF)
                dq = dq + dot_nn(ds, k_ref[keys, :])
                own = pl.ds(0, score_own.shape[1])
                dk_own[own, :] += dot_tn(ds, query)
                dv_own[own, :] += dot_tn(p, d_out)
            dq_ref[spot, :] = (dq * scale).astype(BF)
        dpre_ref[0] = (dk_pre[...] * scale).astype(BF)
        dpre_ref[1] = dv_pre[...].astype(BF)
        dsol_ref[0] = (dk_own[...] * scale).astype(BF)
        dsol_ref[1] = dv_own[...].astype(BF)

    sol = rows - PRE_DEV
    spec = lambda shift: pl.BlockSpec((rows, HEAD_DIM), lambda h, m: (0, h + shift))
    pre = lambda which: pl.BlockSpec((1, prefix, HEAD_DIM), lambda h, m: (which, 0, h))
    both = lambda size: pl.BlockSpec((2, size, HEAD_DIM), lambda h, m: (0, 0, h))
    return pl.pallas_call(
        body,
        grid_spec=pltpu.PrefetchScalarGridSpec(
            num_scalar_prefetch=1,
            grid=(heads,),
            in_specs=[
                spec(0), spec(heads), spec(2 * heads), pre(0), pre(1), spec(0), spec(0),
                pl.BlockSpec((1, rows, 1), lambda h, m: (h, 0, 0)),
            ],
            out_specs=[spec(0), both(prefix), both(sol)],
            scratch_shapes=[
                pltpu.VMEM((prefix, HEAD_DIM), FP),
                pltpu.VMEM((prefix, HEAD_DIM), FP),
                pltpu.VMEM((sol, HEAD_DIM), FP),
                pltpu.VMEM((sol, HEAD_DIM), FP),
            ],
        ),
        out_shape=[
            jax.ShapeDtypeStruct((rows, heads * HEAD_DIM), BF),
            jax.ShapeDtypeStruct((2, prefix, heads * HEAD_DIM), BF),
            jax.ShapeDtypeStruct((2, sol, heads * HEAD_DIM), BF),
        ],
        compiler_params=pltpu.CompilerParams(vmem_limit_bytes=VMEM_LIMIT),
        name="attention_backward",
    )(meta, projected, projected, projected, prefix_kv, prefix_kv, mixed, d_mixed, logs)


def layer_norm(values, gain_row):
    center = values - jnp.mean(values, axis=-1, keepdims=True)
    inverse = lax.rsqrt(jnp.mean(center * center, axis=-1, keepdims=True) + EPS_NORM)
    normal_unit = center * inverse
    return (normal_unit * gain_row, normal_unit, inverse)


def norm_back(incoming, normal_unit, inverse, gain_row):
    scaled = incoming * gain_row
    inner_sum = (
        scaled
        - jnp.mean(scaled, axis=-1, keepdims=True)
        - normal_unit * jnp.mean(scaled * normal_unit, axis=-1, keepdims=True)
    )
    return (inner_sum * inverse, jnp.sum(incoming * normal_unit, axis=0))


def adamw(weight, gradient, moment, variance, average, step_rate, decay_rate):
    moment = BETA_ONE * moment + (1.0 - BETA_ONE) * gradient
    variance = BETA_TWO * variance + (1.0 - BETA_TWO) * gradient * gradient
    corrected = moment / (1.0 - BETA_ONE**STEP)
    scaled_root = jnp.sqrt(variance / (1.0 - BETA_TWO**STEP)) + ADAM_EPS
    weight_new = weight - step_rate * corrected / scaled_root - step_rate * decay_rate * weight
    average = EMA_KEEP * average + (1.0 - EMA_KEEP) * weight_new
    return (moment, variance, weight_new, average)


def after(value, *others):
    return lax.optimization_barrier((value,) + others)[0]


def local(
    seq_count,
    head_count,
    tokens,
    cotangent,
    prefix_length,
    answer_lengths,
    inward,
    outward,
    expand,
    contract,
    norm_gains,
    moment_inward,
    moment_outward,
    moment_expand,
    moment_contract,
    moment_gains,
    variance_inward,
    variance_outward,
    variance_expand,
    variance_contract,
    variance_gains,
    average_inward,
    average_outward,
    average_expand,
    average_contract,
    average_gains,
):
    device = lax.axis_index("seq")
    tok_dev, model = tokens.shape
    share = model // seq_count
    local_width = outward.shape[0]
    limit_prefix = prefix_length[0]
    limit_answer = answer_lengths[0]
    ring = Ring(seq_count)
    team = Team(head_count, tok_dev)
    ids = ring.ids()
    blocks_of = ring.blocks_of()
    meta = jnp.concatenate([jnp.stack([device, limit_prefix, limit_answer]).astype(jnp.int32), ids])
    first = team.first_row()

    in_blocks = ring.gather(inward.astype(BF).reshape(share, 3 * local_width))
    in_matrix = jnp.concatenate(in_blocks, axis=0)
    gain_rows = lax.all_gather(norm_gains.astype(BF), "seq", axis=1, tiled=True)
    gain_pair = jnp.take(gain_rows.reshape(2, seq_count, share), ids, axis=1)
    gain_pair = gain_pair.reshape(2, model).astype(FP)

    source_low = pick_columns(tokens, ids)
    normed_one = layer_norm(source_low.astype(FP), gain_pair[0])[0].astype(BF)
    projected = jnp.dot(normed_one, in_matrix, preferred_element_type=FP).astype(BF)

    own_kv = jnp.stack(
        [
            projected[:PRE_DEV, local_width : 2 * local_width],
            projected[:PRE_DEV, 2 * local_width :],
        ]
    )
    prefix_kv = jnp.concatenate(ring.gather(own_kv), axis=1)
    out_matrix = jnp.concatenate(ring.gather(after(outward, in_blocks[1]).astype(BF)), axis=1)
    up_matrix = jnp.concatenate(ring.gather(after(expand, in_blocks[2]).astype(BF)), axis=0)
    down_matrix = jnp.concatenate(ring.gather(after(contract, in_blocks[3]).astype(BF)), axis=1)
    mixed, logs = attention_forward(meta, projected, prefix_kv)

    def attention_part(start, size):
        return jnp.dot(
            lax.dynamic_slice_in_dim(mixed, start, size, 0), out_matrix, preferred_element_type=FP
        )

    source_own = lax.dynamic_slice_in_dim(source_low, first, team.quarter, 0).astype(FP)
    hidden = source_own + team.scatter_sum(attention_part)
    normed_two_own, unit_two, inverse_two = layer_norm(hidden, gain_pair[1])
    normed_two = team.gather(normed_two_own.astype(BF))
    up_values = jnp.dot(normed_two, up_matrix, preferred_element_type=FP)
    activation_values, gelu_back = jax.vjp(
        lambda entry: jax.nn.gelu(entry, approximate=True), up_values
    )
    activation = activation_values.astype(BF)

    def down_part(start, size):
        return jnp.dot(
            lax.dynamic_slice_in_dim(activation, start, size, 0),
            down_matrix,
            preferred_element_type=FP,
        )

    result = (hidden + team.scatter_sum(down_part)).astype(BF)
    layer_output = pick_columns(team.gather(result), blocks_of)

    position_all = jnp.arange(tok_dev, dtype=jnp.int32)
    valid_rows = jnp.where(
        position_all < PRE_DEV,
        device * PRE_DEV + position_all < limit_prefix,
        position_all - PRE_DEV < limit_answer,
    )
    out_grad = jnp.where(valid_rows[:, None], pick_columns(cotangent, ids), 0).astype(BF)

    def column_block(array, b):
        return array[:, b * share : (b + 1) * share]

    def part_contract(b):
        return jnp.einsum(
            "tf,td->fd", activation, column_block(out_grad, b), preferred_element_type=FP
        )

    red_contract = ring.scatter_sum(part_contract)
    d_activation = jnp.einsum("td,fd->tf", out_grad, down_matrix, preferred_element_type=FP)
    d_up = gelu_back(d_activation)[0].astype(BF)

    def up_back_part(start, size):
        return jnp.einsum(
            "tf,df->td",
            lax.dynamic_slice_in_dim(d_up, start, size, 0),
            up_matrix,
            preferred_element_type=FP,
        )

    d_normed_two = team.scatter_sum(up_back_part)

    def part_expand(b):
        return jnp.einsum(
            "td,tf->df", column_block(normed_two, b), d_up, preferred_element_type=FP
        )

    red_expand = ring.scatter_sum(part_expand)
    d_norm_part, gain_two = norm_back(d_normed_two, unit_two, inverse_two, gain_pair[1])
    out_grad_own = lax.dynamic_slice_in_dim(out_grad, first, team.quarter, 0).astype(FP)
    d_hidden = out_grad_own + d_norm_part
    d_attention = team.gather(d_hidden.astype(BF))
    d_mixed = jnp.einsum("td,nd->tn", d_attention, out_matrix, preferred_element_type=FP).astype(BF)

    def part_outward(b):
        return jnp.einsum(
            "tn,td->nd", mixed, column_block(d_attention, b), preferred_element_type=FP
        )

    red_outward = ring.scatter_sum(part_outward)
    d_query, d_prefix, d_solution = attention_backward(
        meta, projected, prefix_kv, mixed, d_mixed, logs
    )

    def part_prefix(b):
        return d_prefix[:, b * PRE_DEV : (b + 1) * PRE_DEV].astype(FP)

    d_prefix_own = ring.scatter_sum(part_prefix).astype(BF)
    d_kv = jnp.concatenate([d_prefix_own, d_solution], axis=1)
    d_projected = jnp.concatenate([d_query, d_kv[0], d_kv[1]], axis=1)

    def in_back_part(start, size):
        return jnp.einsum(
            "tn,dn->td",
            lax.dynamic_slice_in_dim(d_projected, start, size, 0),
            in_matrix,
            preferred_element_type=FP,
        )

    def part_inward(b):
        return jnp.einsum(
            "td,tn->dn", column_block(normed_one, b), d_projected, preferred_element_type=FP
        )

    red_inward = ring.scatter_sum(part_inward)
    d_normed_one = team.scatter_sum(in_back_part)
    _, unit_one, inverse_one = layer_norm(source_own, gain_pair[0])
    d_source, gain_one = norm_back(d_normed_one, unit_one, inverse_one, gain_pair[0])
    input_low = team.gather((d_hidden + d_source).astype(BF))
    input_grad = pick_columns(input_low, blocks_of).astype(FP)

    gains = jnp.stack([gain_one, gain_two]).reshape(2, seq_count, share)
    gains = jnp.take(gains, blocks_of, axis=1)
    gains = total_of_all(gains, seq_count, head_count)
    red_gains = lax.dynamic_slice_in_dim(gains, device, 1, 1)[:, 0]
    squares = total_of_all(
        jnp.sum(red_inward * red_inward)
        + jnp.sum(red_outward * red_outward)
        + jnp.sum(red_expand * red_expand)
        + jnp.sum(red_contract * red_contract),
        seq_count,
        head_count,
    )
    grad_norm = jnp.sqrt(squares + jnp.sum(gains * gains))
    factor = CLIP_NORM / jnp.maximum(grad_norm, CLIP_NORM)

    in_new = adamw(
        inward, red_inward.reshape(inward.shape) * factor, moment_inward, variance_inward,
        average_inward, RATE_INWARD, DECAY_MATRIX,
    )
    out_new = adamw(
        outward, red_outward * factor, moment_outward, variance_outward, average_outward,
        RATE_OUTWARD, DECAY_MATRIX,
    )
    up_new = adamw(
        expand, red_expand * factor, moment_expand, variance_expand, average_expand,
        RATE_EXPAND, DECAY_MATRIX,
    )
    down_new = adamw(
        contract, red_contract * factor, moment_contract, variance_contract, average_contract,
        RATE_CONTRACT, DECAY_MATRIX,
    )
    gain_new = adamw(
        norm_gains, red_gains * factor, moment_gains, variance_gains, average_gains, RATE_GAINS, 0.0
    )
    return (
        (layer_output, input_grad, jnp.reshape(grad_norm, (1,)))
        + in_new + out_new + up_new + down_new + gain_new
    )


def solution(mesh):
    in_place = P("seq", None, "head")
    out_place = P("head", "seq")
    up_place = P("seq", "head")
    gain_place = P(None, "seq")
    weights = (in_place, out_place, up_place, out_place, gain_place)
    placed = (P("seq", None), P("seq", None), P(), P("seq")) + weights * 4
    results = (P("seq", None), P("seq", None), P())
    for place in weights:
        results += (place,) * 4
    return jax.shard_map(
        functools.partial(local, mesh.shape["seq"], mesh.shape["head"]),
        mesh=mesh,
        in_specs=placed,
        out_specs=results,
        check_vma=False,
    )
```

```python
import functools

import jax
import jax.numpy as jnp
from jax import lax
from jax.experimental import pallas as pl
from jax.experimental.pallas import tpu as pltpu
from jax.sharding import PartitionSpec as P

HEAD_DIM = 128
PRE_DEV = 256
SOL_DEV = 768
STEP = 10
BLOCK = 256

EPS_NORM = 1e-05
BETA_ONE = 0.9
BETA_TWO = 0.95
ADAM_EPS = 1e-08
EMA_KEEP = 0.7
CLIP_NORM = 1.0
DECAY_MATRIX = 0.1
RATE_INWARD = 0.05
RATE_OUTWARD = 0.15
RATE_EXPAND = 0.05
RATE_CONTRACT = 0.03
RATE_GAINS = 0.5

LOG2E = 1.4426950408889634
MASKED = -1e30
BF = jnp.bfloat16
FP = jnp.float32
VMEM_LIMIT = 56 * 1024 * 1024


def ring_order(count):
    depth = 4
    if count % depth or (count // depth) % 2:
        return list(range(count))
    width = count // depth
    order = [z * width for z in range(depth)]
    across = list(range(1, width))
    for z in reversed(range(depth)):
        order += [z * width + y for y in across]
        across = across[::-1]
    return order


class Ring:
    def __init__(self, count):
        self.count = count
        self.half = count // 2
        self.order = ring_order(count)
        self.up = [(self.order[i], self.order[(i + 1) % count]) for i in range(count)]
        self.down = [(b, a) for a, b in self.up]
        inverse = [0] * count
        for i, s in enumerate(self.order):
            inverse[s] = i
        self.inverse = inverse

    def gather(self, own):
        return Gather(self, own)

    def scatter(self, far):
        return Scatter(self, far)


class Gather:
    def __init__(self, ring, own):
        self.ring = ring
        self.blocks = [None] * ring.count
        self.blocks[0] = own
        self.fresh = [own, own]
        self.done = 0
        self.advance()

    def advance(self):
        ring = self.ring
        self.done += 1
        upper, lower = self.fresh
        if self.done == ring.half:
            mid = upper.shape[0] // 2
            upper, lower = upper[:mid], lower[mid:]
        self.fresh = [
            lax.ppermute(upper, "seq", ring.down),
            lax.ppermute(lower, "seq", ring.up),
        ]
        self.waiting = True

    def complete(self):
        while True:
            if self.waiting:
                pin([self])
            if self.done == self.ring.half:
                return self.blocks
            self.advance()

    def arrive(self):
        self.waiting = False
        j, n = self.done, self.ring.count
        if j == self.ring.half:
            self.blocks[j] = jnp.concatenate(self.fresh, axis=0)
        else:
            self.blocks[j], self.blocks[n - j] = self.fresh


class Scatter:
    def __init__(self, ring, far):
        self.ring = ring
        self.mid = far.shape[0] // 2
        self.left = ring.half
        self.send(far[: self.mid].astype(BF), far[self.mid :].astype(BF))

    def send(self, rising, falling):
        self.left -= 1
        self.fresh = [
            lax.ppermute(rising, "seq", self.ring.up),
            lax.ppermute(falling, "seq", self.ring.down),
        ]

    def arrive(self):
        pass

    def advance(self, part, order):
        j, mid = self.left, self.mid
        rising, falling = self.fresh
        upper, lower = part(j), part(self.ring.count - j)
        if j == self.ring.half - 1:
            upper = jnp.concatenate([upper[:mid] + rising.astype(FP), upper[mid:]], axis=0)
            lower = jnp.concatenate([lower[:mid], lower[mid:] + falling.astype(FP)], axis=0)
        else:
            upper = upper + rising.astype(FP)
            lower = lower + falling.astype(FP)
        order.upper, order.lower = upper.astype(BF), lower.astype(BF)
        order.pin()
        self.send(order.out.upper, order.out.lower)

    def finish(self, part, order):
        while self.left:
            order.pin(self)
            self.advance(part, order)
        return part(0) + self.fresh[0].astype(FP) + self.fresh[1].astype(FP)


class Team:
    def __init__(self, count):
        self.cores = 2 if count % 2 == 0 else 1
        self.chips = count // self.cores
        self.count = count
        self.core_flip = [(i, i ^ 1) for i in range(count)]

    def quarters(self, index):
        x, c = index // self.cores, index % self.cores
        cores = [c] + [1 - c] * (self.cores - 1)
        return [k * self.chips + (x + i) % self.chips for k in cores for i in range(self.chips)]

    def shift(self, k):
        chips, cores = self.chips, self.cores
        return [
            (x * cores + c, ((x + k) % chips) * cores + c) for x in range(chips) for c in range(cores)
        ]

    def cross(self, away):
        return lax.ppermute(away, "head", self.core_flip) if self.cores == 2 else None

    def send_sums(self, kept, got):
        size = kept.shape[0] // self.chips
        arrived = []
        for k in range(1, self.chips):
            spot = slice(k * size, (k + 1) * size)
            term = kept[spot].astype(FP)
            if got is not None:
                term = term + got[spot].astype(FP)
            arrived.append(lax.ppermute(term.astype(BF), "head", self.shift(k)))
        return arrived

    def send_own(self, own):
        return [own] + [lax.ppermute(own, "head", self.shift(-k)) for k in range(1, self.chips)]

    def send_half(self, parts):
        if self.cores == 1:
            return list(parts)
        half = jnp.concatenate(parts, axis=0) if self.chips > 1 else parts[0]
        return list(parts) + [lax.ppermute(half, "head", self.core_flip)]


def total_of_all(value, seq_count, head_count):
    for axis, count in (("head", head_count), ("seq", seq_count)):
        step = 1
        while step < count:
            value = value + lax.ppermute(value, axis, [(i, i ^ step) for i in range(count)])
            step *= 2
    return value


PARAMS = pltpu.CompilerParams(vmem_limit_bytes=VMEM_LIMIT)
ANYWHERE = pl.BlockSpec(memory_space=pl.ANY)
META_IDS = 3


def dot_nt(a, b):
    return lax.dot_general(a, b, (((1,), (1,)), ((), ())), preferred_element_type=FP)


def dot_nn(a, b):
    return lax.dot_general(a, b, (((1,), (0,)), ((), ())), preferred_element_type=FP)


def dot_tn(a, b):
    return lax.dot_general(a, b, (((0,), (0,)), ((), ())), preferred_element_type=FP)


def lanes(index, size):
    return pl.ds(pl.multiple_of(index * size, size), size)


def unit_of(values):
    center = values - jnp.mean(values, axis=-1, keepdims=True)
    inverse = lax.rsqrt(jnp.mean(center * center, axis=-1, keepdims=True) + EPS_NORM)
    return center * inverse, inverse


def norm_back(incoming, unit, inverse, gain_row):
    scaled = incoming * gain_row
    inner = (
        scaled
        - jnp.mean(scaled, axis=-1, keepdims=True)
        - unit * jnp.mean(scaled * unit, axis=-1, keepdims=True)
    )
    return inner * inverse, jnp.sum(incoming * unit, axis=0, keepdims=True)


def call(body, name, meta, inputs, in_specs, out_specs, out_shape, grid=(1,), scratch=()):
    return pl.pallas_call(
        body,
        grid_spec=pltpu.PrefetchScalarGridSpec(
            num_scalar_prefetch=1,
            grid=grid,
            in_specs=in_specs,
            out_specs=out_specs,
            scratch_shapes=list(scratch),
        ),
        out_shape=out_shape,
        compiler_params=PARAMS,
        cost_estimate=pl.CostEstimate(flops=1, bytes_accessed=1, transcendentals=0),
        name=name,
    )(meta, *inputs)


def first_norm(meta, tokens, gains, rows, n):
    model = tokens.shape[1]
    share = model // n

    def body(meta_ref, in_ref, gain_ref, norm_ref, source_ref, held):
        held[...], _ = unit_of(in_ref[...].astype(FP))
        for b in range(n):
            here = pl.ds(b * share, share)
            there = lanes(meta_ref[META_IDS + b], share)
            norm_ref[:, here] = (held[:, there] * gain_ref[0:1, here]).astype(BF)
            source_ref[:, here] = in_ref[:, there]

    tile = pl.BlockSpec((BLOCK, model), lambda i, m: (i, 0))
    return call(
        body, "first_norm", meta, (tokens, gains),
        [tile, pl.BlockSpec((2, model), lambda i, m: (0, 0))], [tile, tile],
        [jax.ShapeDtypeStruct((rows, model), BF), jax.ShapeDtypeStruct((rows, model), BF)],
        grid=(rows // BLOCK,),
        scratch=[pltpu.VMEM((BLOCK, model), FP)],
    )


def mask_cotangent(meta, cotangent, n, m):
    rows, model = cotangent.shape
    share, quarter = model // n, rows // m

    def body(meta_ref, in_ref, out_ref):
        spot = meta_ref[META_IDS + n + pl.program_id(0)] * quarter
        row = lax.broadcasted_iota(jnp.int32, (quarter, share), 0) + spot
        limit = jnp.where(
            row < PRE_DEV, meta_ref[1] - meta_ref[0] * PRE_DEV, meta_ref[2] + PRE_DEV
        )
        for b in range(n):
            piece = in_ref[:, lanes(meta_ref[META_IDS + b], share)]
            out_ref[:, pl.ds(b * share, share)] = jnp.where(row < limit, piece.astype(FP), 0).astype(BF)

    return call(
        body, "mask_cotangent", meta, (cotangent,),
        [pl.BlockSpec((quarter, model), lambda i, meta: (meta[META_IDS + n + i], 0))],
        pl.BlockSpec((quarter, model), lambda i, meta: (i, 0)),
        jax.ShapeDtypeStruct((rows, model), BF),
        grid=(m,),
    )


def place_rows(meta, pieces, n, m, dtype):
    quarter, model = pieces[0].shape
    share = model // n
    count = len(pieces)
    starts = [0]
    for piece in pieces:
        starts.append(starts[-1] + piece.shape[0] // quarter)

    def body(meta_ref, *refs):
        out_ref = refs[count]
        for k in range(count):

            @pl.when((pl.program_id(0) >= starts[k]) & (pl.program_id(0) < starts[k + 1]))
            def _():
                for b in range(n):
                    out_ref[:, lanes(meta_ref[META_IDS + b], share)] = refs[k][
                        :, pl.ds(b * share, share)
                    ].astype(dtype)

    def spec(k):
        last = starts[k + 1] - starts[k] - 1
        return pl.BlockSpec(
            (quarter, model), lambda i, meta: (jnp.clip(i - starts[k], 0, last), 0)
        )

    return call(
        body, "place_rows", meta, pieces, [spec(k) for k in range(count)],
        pl.BlockSpec((quarter, model), lambda i, meta: (meta[META_IDS + n + i], 0)),
        jax.ShapeDtypeStruct((quarter * m, model), dtype),
        grid=(m,),
    )


def project_prefix(meta, normed, weights, out_shard):
    n = len(weights)
    model = normed.shape[1]
    width = weights[0].shape[1]
    share = model // n

    def body(meta_ref, x_ref, shard_ref, *refs):
        blocks, (send_ref, held, sems) = refs[:n], refs[n:]

        def copy(b):
            return pltpu.make_async_copy(
                blocks[b].at[pl.ds(share, 2 * share), :], held.at[b], sems.at[b]
            )

        for b in range(n):
            copy(b).start()
        send_ref[pl.ds(2 * PRE_DEV, share), :] = shard_ref[...]
        totals = [None, None]
        for b in range(n):
            copy(b).wait()
            for c in range(2):
                term = dot_nn(
                    x_ref[:, pl.ds(b * share, share)], held[b, pl.ds(c * share, share), :]
                )
                totals[c] = term if b == 0 else totals[c] + term
        for c in range(2):
            send_ref[pl.ds(c * PRE_DEV, PRE_DEV), :] = totals[c].astype(BF)

    sent = 2 * PRE_DEV + share
    return call(
        body, "project_prefix", meta, (normed, out_shard, *weights),
        [
            pl.BlockSpec((PRE_DEV, model), lambda i, m: (0, 0)),
            pl.BlockSpec((share, width), lambda i, m: (0, 0)),
        ]
        + [ANYWHERE] * n,
        pl.BlockSpec((sent, width), lambda i, m: (0, 0)),
        jax.ShapeDtypeStruct((sent, width), BF),
        scratch=[pltpu.VMEM((n, 2 * share, width), BF), pltpu.SemaphoreType.DMA((n,))],
    )


def project(meta, normed, weights):
    n = len(weights)
    rows, model = normed.shape
    width = weights[0].shape[1]
    share = model // n

    def body(meta_ref, x_ref, *refs):
        blocks, (out_ref, held, sems) = refs[:n], refs[n:]
        part = pl.program_id(0)

        def copy(c, b):
            return pltpu.make_async_copy(
                blocks[b].at[pl.ds(pl.multiple_of(c * share, share), share), :],
                held.at[c, pl.ds(b * share, share), :],
                sems.at[c, b],
            )

        @pl.when(part == 0)
        def _():
            for c in range(3):
                for b in range(n):
                    copy(c, b).start()

        for b in range(n):
            copy(part, b).wait()
        out_ref[0] = dot_nn(x_ref[...], held[part]).astype(BF)

    return call(
        body, "project", meta, (normed, *weights),
        [pl.BlockSpec((rows, model), lambda c, m: (0, 0))] + [ANYWHERE] * n,
        pl.BlockSpec((1, rows, width), lambda c, m: (c, 0, 0)),
        jax.ShapeDtypeStruct((3, rows, width), BF),
        grid=(3,),
        scratch=[pltpu.VMEM((3, model, width), BF), pltpu.SemaphoreType.DMA((3, n))],
    )


def rows_matmul(meta, name, x, weights, m, placed, taken, form, layer=None):
    n = len(weights)
    rows, depth = x.shape[-2:]
    quarter = rows // m
    kept = quarter * (m // 2) if m % 2 == 0 else rows
    offset, size = taken
    width = weights[0].shape[1]
    held_rows = weights[0].shape[0] if size is None else size
    column = {"nn": width, "nt": held_rows}.get(form, held_rows // 3)
    group = max(1, min(n, 512 // column))
    tile = group * column
    steps = n // group

    def body(meta_ref, x_any, *refs):
        blocks, outs = refs[:n], refs[n:-4]
        x_held, held, x_sems, sems = refs[-4:]
        step = pl.program_id(0)

        def x_copy(i):
            spot = i * quarter
            if placed:
                spot = pl.multiple_of(meta_ref[META_IDS + n + i] * quarter, quarter)
            x_rows = x_any if layer is None else x_any.at[layer]
            return pltpu.make_async_copy(
                x_rows.at[pl.ds(spot, quarter), :],
                x_held.at[pl.ds(i * quarter, quarter), :],
                x_sems.at[i],
            )

        def copies(s, g):
            block = blocks[s * group + g]
            sem = sems.at[s, g]
            if form == "three":
                return [
                    pltpu.make_async_copy(
                        block.at[pl.ds(c * column, column), :],
                        held.at[s, pl.ds(g * column, column), pl.ds(c * width, width)],
                        sems.at[s, g * 3 + c],
                    )
                    for c in range(3)
                ]
            source = block if size is None else block.at[pl.ds(offset, size), :]
            if form == "nn":
                target = held.at[s, :, pl.ds(g * column, column)]
            else:
                target = held.at[s, pl.ds(g * column, column), :]
            return [pltpu.make_async_copy(source, target, sem)]

        @pl.when(step == 0)
        def _():
            for i in range(m):
                x_copy(i).start()
            for s in range(steps):
                for g in range(group):
                    for one in copies(s, g):
                        one.start()
            for i in range(m):
                x_copy(i).wait()

        for s in range(steps):

            @pl.when(step == s)
            def _():
                for g in range(group):
                    for one in copies(s, g):
                        one.wait()

        product = (dot_nn if form == "nn" else dot_nt)(x_held[...], held[step]).astype(BF)
        outs[0][...] = product[:kept]
        if kept < rows:
            outs[1][...] = product[kept:]

    if form == "nn":
        held_shape = (steps, depth, tile)
    else:
        held_shape = (steps, tile, depth)
    sizes = [kept] + ([rows - kept] if kept < rows else [])
    return call(
        body, name, meta, (x, *weights), [ANYWHERE] * (n + 1),
        [pl.BlockSpec((size_of, tile), lambda s, m: (0, s)) for size_of in sizes],
        [jax.ShapeDtypeStruct((size_of, n * column), BF) for size_of in sizes],
        grid=(steps,),
        scratch=[
            pltpu.VMEM((rows, depth), BF),
            pltpu.VMEM(held_shape, BF),
            pltpu.SemaphoreType.DMA((m,)),
            pltpu.SemaphoreType.DMA((steps, 3 * group if form == "three" else group)),
        ],
    )


def tile_of(width):
    return min(512, width)


def feed_back(meta, out_grad, weights):
    n = len(weights)
    rows, model = out_grad.shape
    width, share = weights[0].shape
    tile = tile_of(width)
    tiles = width // tile

    def body(meta_ref, x_ref, *refs):
        blocks, (out_ref, held, sems) = refs[:n], refs[n:]
        step = pl.program_id(0)

        def copy(t, b):
            return pltpu.make_async_copy(
                blocks[b].at[pl.ds(pl.multiple_of(t * tile, tile), tile), :],
                held.at[t, :, pl.ds(b * share, share)],
                sems.at[t, b],
            )

        @pl.when(step == 0)
        def _():
            for t in range(tiles):
                for b in range(n):
                    copy(t, b).start()

        for b in range(n):
            copy(step, b).wait()
        out_ref[...] = dot_nt(x_ref[...], held[step]).astype(BF)

    part = pl.BlockSpec((rows, tile), lambda t, m: (0, t))
    return call(
        body, "feed_back", meta, (out_grad, *weights),
        [pl.BlockSpec((rows, model), lambda t, m: (0, 0))] + [ANYWHERE] * n,
        part,
        jax.ShapeDtypeStruct((rows, width), BF),
        grid=(tiles,),
        scratch=[pltpu.VMEM((tiles, tile, model), BF), pltpu.SemaphoreType.DMA((tiles, n))],
    )


def feed_up(meta, pieces, weights, d_activation):
    n, count = len(weights), len(pieces)
    rows = sum(piece.shape[0] for piece in pieces)
    model = pieces[0].shape[1]
    width = weights[0].shape[1]
    share = model // n
    tile = tile_of(width)
    tiles = width // tile
    root = 0.7978845608028654
    step_rows = 512

    def body(meta_ref, *refs):
        parts, blocks, back_ref = refs[:count], refs[count : count + n], refs[count + n]
        x_out, both_ref, held, sems, x_sems = refs[count + n + 1 :]
        step = pl.program_id(0)

        def copy(t, b):
            return pltpu.make_async_copy(
                blocks[b].at[:, lanes(t, tile)],
                held.at[t, pl.ds(b * share, share), :],
                sems.at[t, b],
            )

        def x_copies():
            at, copies = 0, []
            for k in range(count):
                size = pieces[k].shape[0]
                copies.append(
                    pltpu.make_async_copy(parts[k], x_out.at[pl.ds(at, size), :], x_sems.at[k])
                )
                at += size
            return copies

        @pl.when(step == 0)
        def _():
            for one in x_copies():
                one.start()
            for t in range(tiles):
                for b in range(n):
                    copy(t, b).start()
            for one in x_copies():
                one.wait()

        for b in range(n):
            copy(step, b).wait()

        for i in range(rows // step_rows):
            spot = pl.ds(i * step_rows, step_rows)
            v = dot_nn(x_out[spot, :], held[step])
            square = v * v
            t = jnp.tanh(root * v * (1.0 + 0.044715 * square))
            half = 0.5 * (1.0 + t)
            both_ref[0, spot, :] = (v * half).astype(BF)
            slope = half + 0.5 * v * (1.0 - t * t) * (root * (1.0 + 3.0 * 0.044715 * square))
            both_ref[1, spot, :] = (back_ref[spot, :].astype(FP) * slope).astype(BF)

    return call(
        body, "feed_up", meta, (*pieces, *weights, d_activation),
        [ANYWHERE] * (count + n) + [pl.BlockSpec((rows, tile), lambda t, m: (0, t))],
        [
            pl.BlockSpec((rows, model), lambda t, m: (0, 0)),
            pl.BlockSpec((2, rows, tile), lambda t, m: (0, 0, t)),
        ],
        [
            jax.ShapeDtypeStruct((rows, model), BF),
            jax.ShapeDtypeStruct((2, rows, width), BF),
        ],
        grid=(tiles,),
        scratch=[
            pltpu.VMEM((tiles, model, tile), BF),
            pltpu.SemaphoreType.DMA((tiles, n)),
            pltpu.SemaphoreType.DMA((count,)),
        ],
    )


def feed_terms(meta, out_grad, normed, both, blocks, received, n, dtype, cut=False):
    rows, model = out_grad.shape
    width = both.shape[2]
    share = model // n
    count = len(blocks)
    flat = [(k, array, start) for k, sums in enumerate(received) for array, start in sums]

    def body(meta_ref, grad_ref, norm_ref, both_ref, *refs):
        arrived, outs = refs[: len(flat)], refs[len(flat) :]
        matrix, block = pl.program_id(0), pl.program_id(1)
        for k in range(count):
            for which, left in ((0, grad_ref), (1, norm_ref)):

                @pl.when((matrix == which) & (block == k))
                def _():
                    term = dot_tn(left[...], both_ref[0])
                    for (at, array, start), ref in zip(flat, arrived):
                        if at == k and start <= which < start + array.shape[0] // share:
                            term = term + ref[...].astype(FP)
                    outs[which if cut else k][...] = term.astype(dtype)

    def chosen(k):
        b = blocks[0]
        for i in range(1, count):
            b = jnp.where(k == i, blocks[i], b)
        return b

    def received_spec(array, start):
        last = array.shape[0] // share - 1
        return pl.BlockSpec((share, width), lambda t, k, m: (jnp.clip(t - start, 0, last), 0))

    column = pl.BlockSpec((rows, share), lambda t, k, m: (0, chosen(k)))
    out = call(
        body, "feed_terms", meta, (out_grad, normed, both, *[array for _, array, _ in flat]),
        [column, column, pl.BlockSpec((1, rows, width), lambda t, k, m: (t, 0, 0))]
        + [received_spec(array, start) for _, array, start in flat],
        [pl.BlockSpec((share, width), lambda t, k, m: (0 if cut else t, 0))] * (2 if cut else count),
        [jax.ShapeDtypeStruct(((1 if cut else 2) * share, width), dtype)] * (2 if cut else count),
        grid=(2, count),
    )
    return out


def mixed_back(meta, pieces, weights, mixed, offset, n, m):
    count = len(pieces)
    quarter, model = pieces[0].shape
    share = model // n
    rows, width = mixed.shape

    def body(meta_ref, *refs):
        parts, blocks, mixed_ref = refs[:count], refs[count : count + n], refs[count + n]
        x_out, d_ref, mixed_out, held, sems, x_sems = refs[count + n + 1 :]
        step = pl.program_id(0)

        def copy(b):
            return pltpu.make_async_copy(
                blocks[b].at[pl.ds(offset, share), :],
                held.at[pl.ds(b * share, share), :],
                sems.at[b],
            )

        def x_copies():
            at, copies = 0, []
            for k in range(count):
                size = pieces[k].shape[0]
                copies.append(
                    pltpu.make_async_copy(parts[k], x_out.at[pl.ds(at, size), :], x_sems.at[k])
                )
                at += size
            return copies

        @pl.when(step == 0)
        def _():
            for one in x_copies() + [copy(b) for b in range(n)]:
                one.start()
            for one in x_copies() + [copy(b) for b in range(n)]:
                one.wait()

        spot = pl.ds(pl.multiple_of(step * quarter, quarter), quarter)
        d_ref[...] = dot_nn(x_out[spot, :], held[...]).astype(BF)
        mixed_out[...] = mixed_ref[...]

    placed = pl.BlockSpec((quarter, width), lambda i, meta: (meta[META_IDS + n + i], 0))
    return call(
        body, "mixed_back", meta, (*pieces, *weights, mixed),
        [ANYWHERE] * (count + n) + [placed],
        [
            pl.BlockSpec((rows, model), lambda i, meta: (0, 0)),
            placed,
            pl.BlockSpec((quarter, width), lambda i, meta: (i, 0)),
        ],
        [
            jax.ShapeDtypeStruct((rows, model), BF),
            jax.ShapeDtypeStruct((rows, width), BF),
            jax.ShapeDtypeStruct((rows, width), BF),
        ],
        grid=(m,),
        scratch=[
            pltpu.VMEM((model, width), BF),
            pltpu.SemaphoreType.DMA((n,)),
            pltpu.SemaphoreType.DMA((count,)),
        ],
    )


def own_quarter(quarter, model, step):
    steps = quarter // step
    plain = pl.BlockSpec((step, model), lambda i, meta: (i, 0))
    whole = pl.BlockSpec((2, model), lambda i, meta: (0, 0))

    def placed(n):
        return pl.BlockSpec(
            (step, model), lambda i, meta: (meta[META_IDS + n] * steps + i, 0)
        )

    return steps, plain, whole, placed


def second_norm(meta, terms, source, gains, quarter, n):
    model = source.shape[1]
    steps, plain, whole, placed = own_quarter(quarter, model, min(64, quarter))
    count = len(terms)

    def body(meta_ref, *refs):
        source_ref, gain_ref, hidden_ref, norm_ref = refs[count:]
        hidden = refs[0][...].astype(FP)
        for k in range(1, count):
            hidden = hidden + refs[k][...].astype(FP)
        hidden = source_ref[...].astype(FP) + hidden
        hidden_ref[...] = hidden
        norm_ref[...] = (unit_of(hidden)[0] * gain_ref[1:2, :]).astype(BF)

    return call(
        body, "second_norm", meta, (*terms, source, gains),
        [plain] * count + [placed(n), whole], [plain, plain],
        [jax.ShapeDtypeStruct((quarter, model), FP), jax.ShapeDtypeStruct((quarter, model), BF)],
        grid=(steps,),
    )


def second_norm_back(meta, terms, hidden, out_grad, gains):
    quarter, model = hidden.shape
    steps, plain, whole, _ = own_quarter(quarter, model, min(64, quarter))
    count = len(terms)

    def body(meta_ref, *refs):
        hidden_ref, grad_ref, gain_ref, d_ref, low_ref, dg_ref = refs[count:]
        incoming = refs[0][...].astype(FP)
        for k in range(1, count):
            incoming = incoming + refs[k][...].astype(FP)
        unit, inverse = unit_of(hidden_ref[...])
        d_norm, d_gain = norm_back(incoming, unit, inverse, gain_ref[1:2, :])
        d_hidden = grad_ref[...].astype(FP) + d_norm
        d_ref[...] = d_hidden
        low_ref[...] = d_hidden.astype(BF)

        @pl.when(pl.program_id(0) == 0)
        def _():
            dg_ref[...] = d_gain

        @pl.when(pl.program_id(0) > 0)
        def _():
            dg_ref[...] += d_gain

    return call(
        body, "second_norm_back", meta, (*terms, hidden, out_grad, gains),
        [plain] * (count + 2) + [whole],
        [plain, plain, pl.BlockSpec((1, model), lambda i, m: (0, 0))],
        [
            jax.ShapeDtypeStruct((quarter, model), FP),
            jax.ShapeDtypeStruct((quarter, model), BF),
            jax.ShapeDtypeStruct((1, model), FP),
        ],
        grid=(steps,),
    )


def first_norm_back(meta, terms, source, d_hidden, gains, n):
    quarter, model = d_hidden.shape
    steps, plain, whole, placed = own_quarter(quarter, model, min(64, quarter))
    count = len(terms)

    def body(meta_ref, *refs):
        source_ref, hidden_ref, gain_ref, low_ref, dg_ref = refs[count:]
        incoming = refs[0][...].astype(FP)
        for k in range(1, count):
            incoming = incoming + refs[k][...].astype(FP)
        unit, inverse = unit_of(source_ref[...].astype(FP))
        d_norm, d_gain = norm_back(incoming, unit, inverse, gain_ref[0:1, :])
        low_ref[...] = (hidden_ref[...] + d_norm).astype(BF)

        @pl.when(pl.program_id(0) == 0)
        def _():
            dg_ref[...] = d_gain

        @pl.when(pl.program_id(0) > 0)
        def _():
            dg_ref[...] += d_gain

    return call(
        body, "first_norm_back", meta, (*terms, source, d_hidden, gains),
        [plain] * count + [placed(n), plain, whole],
        [plain, pl.BlockSpec((1, model), lambda i, m: (0, 0))],
        [jax.ShapeDtypeStruct((quarter, model), BF), jax.ShapeDtypeStruct((1, model), FP)],
        grid=(steps,),
    )


def prefix_places(meta_ref, n):
    spot = lax.broadcasted_iota(jnp.int32, (1, PRE_DEV), 1)
    return jnp.concatenate([spot + meta_ref[META_IDS + b] * PRE_DEV for b in range(n)], axis=1)


def masked_scores(meta_ref, q_ref, k_ref, kp_ref, places, block):
    limit_prefix = meta_ref[1]
    limit_answer = meta_ref[2]
    query = q_ref[0, pl.ds(block * BLOCK, BLOCK), :]
    score_pre = dot_nt(query, kp_ref[...])
    if block < PRE_DEV // BLOCK:
        row = lax.broadcasted_iota(jnp.int32, (BLOCK, 1), 0) + block * BLOCK
        reach = jnp.minimum(meta_ref[0] * PRE_DEV + row + 1, limit_prefix)
        return query, jnp.where(places < reach, score_pre, MASKED), None
    score_pre = jnp.where(places < limit_prefix, score_pre, MASKED)
    solution_row = block * BLOCK - PRE_DEV
    width = solution_row + BLOCK
    score_own = dot_nt(query, k_ref[0, pl.ds(PRE_DEV, width), :])
    row = lax.broadcasted_iota(jnp.int32, (BLOCK, 1), 0) + solution_row
    reach = jnp.minimum(row + 1, limit_answer)
    column = lax.broadcasted_iota(jnp.int32, (1, width), 1)
    return query, score_pre, jnp.where(column < reach, score_own, MASKED)


def attention_specs(rows, n):
    part = lambda c: pl.BlockSpec((1, rows, HEAD_DIM), lambda h, m: (c, 0, h))
    pre = lambda c: pl.BlockSpec((PRE_DEV, HEAD_DIM), lambda h, m: (c, h))
    return [part(0), part(1), part(2)] + [pre(0)] * n + [pre(1)] * n


def attention_forward(meta, projected, prefix_kv):
    _, rows, width = projected.shape
    heads = width // HEAD_DIM
    n = len(prefix_kv)
    prefix = n * PRE_DEV
    scale = HEAD_DIM ** (-0.5) * LOG2E

    def body(meta_ref, q_ref, k_ref, v_ref, *refs):
        keys, values, (out_ref, log_ref, kp_ref, vp_ref) = refs[:n], refs[n : 2 * n], refs[2 * n :]
        for b in range(n):
            kp_ref[pl.ds(b * PRE_DEV, PRE_DEV), :] = keys[b][...]
            vp_ref[pl.ds(b * PRE_DEV, PRE_DEV), :] = values[b][...]
        places = prefix_places(meta_ref, n)
        for block in range(rows // BLOCK):
            _, score_pre, score_own = masked_scores(meta_ref, q_ref, k_ref, kp_ref, places, block)
            top = jnp.max(score_pre, axis=-1, keepdims=True)
            if score_own is not None:
                top = jnp.maximum(top, jnp.max(score_own, axis=-1, keepdims=True))
            e_pre = jnp.exp2((score_pre - top) * scale)
            total = jnp.sum(e_pre, axis=-1, keepdims=True)
            out = dot_nn(e_pre.astype(BF), vp_ref[...])
            if score_own is not None:
                e_own = jnp.exp2((score_own - top) * scale)
                total = total + jnp.sum(e_own, axis=-1, keepdims=True)
                out = out + dot_nn(
                    e_own.astype(BF), v_ref[0, pl.ds(PRE_DEV, score_own.shape[1]), :]
                )
            out_ref[pl.ds(block * BLOCK, BLOCK), :] = (out / total).astype(BF)
            log_ref[0, pl.ds(block * BLOCK, BLOCK), :] = top * scale + jnp.log2(total)

    return call(
        body, "attention_forward", meta, (projected,) * 3 + tuple(prefix_kv) * 2,
        attention_specs(rows, n),
        [
            pl.BlockSpec((rows, HEAD_DIM), lambda h, m: (0, h)),
            pl.BlockSpec((1, rows, 1), lambda h, m: (h, 0, 0)),
        ],
        [
            jax.ShapeDtypeStruct((rows, heads * HEAD_DIM), BF),
            jax.ShapeDtypeStruct((heads, rows, 1), FP),
        ],
        grid=(heads,),
        scratch=[pltpu.VMEM((prefix, HEAD_DIM), BF), pltpu.VMEM((prefix, HEAD_DIM), BF)],
    )


def attention_backward(meta, projected, prefix_kv, mixed, d_mixed, logs, d_out_matrix):
    _, rows, width = projected.shape
    heads = width // HEAD_DIM
    n = len(prefix_kv)
    prefix = n * PRE_DEV
    share = d_out_matrix.shape[0] // n
    scale = HEAD_DIM ** (-0.5)
    sent = 2 * PRE_DEV + share

    def body(meta_ref, q_ref, k_ref, v_ref, *refs):
        keys, values = refs[:n], refs[n : 2 * n]
        o_ref, do_ref, log_ref, matrix_ref, d_ref, send_ref = refs[2 * n : 2 * n + 6]
        kp_ref, vp_ref, dk_pre, dv_pre, dk_own, dv_own = refs[2 * n + 6 :]
        for b in range(n):
            kp_ref[pl.ds(b * PRE_DEV, PRE_DEV), :] = keys[b][...]
            vp_ref[pl.ds(b * PRE_DEV, PRE_DEV), :] = values[b][...]
            send_ref[b, pl.ds(2 * PRE_DEV, share), :] = matrix_ref[pl.ds(b * share, share), :]
        places = prefix_places(meta_ref, n)
        dk_own[...] = jnp.zeros_like(dk_own)
        dv_own[...] = jnp.zeros_like(dv_own)
        for block in range(rows // BLOCK):
            spot = pl.ds(block * BLOCK, BLOCK)
            query, score_pre, score_own = masked_scores(
                meta_ref, q_ref, k_ref, kp_ref, places, block
            )
            d_out = do_ref[spot, :]
            log = log_ref[0, spot, :]
            inner = jnp.sum(d_out.astype(FP) * o_ref[spot, :].astype(FP), axis=-1, keepdims=True)
            p = jnp.exp2(score_pre * (scale * LOG2E) - log)
            ds = (p * (dot_nt(d_out, vp_ref[...]) - inner)).astype(BF)
            p = p.astype(BF)
            dq = dot_nn(ds, kp_ref[...])
            dk_term = dot_tn(ds, query)
            dv_term = dot_tn(p, d_out)
            if block == 0:
                dk_pre[...] = dk_term
                dv_pre[...] = dv_term
            else:
                dk_pre[...] += dk_term
                dv_pre[...] += dv_term
            if score_own is not None:
                near = pl.ds(PRE_DEV, score_own.shape[1])
                p = jnp.exp2(score_own * (scale * LOG2E) - log)
                ds = (p * (dot_nt(d_out, v_ref[0, near, :]) - inner)).astype(BF)
                p = p.astype(BF)
                dq = dq + dot_nn(ds, k_ref[0, near, :])
                own = pl.ds(0, score_own.shape[1])
                dk_own[own, :] += dot_tn(ds, query)
                dv_own[own, :] += dot_tn(p, d_out)
            d_ref[0, spot, :] = (dq * scale).astype(BF)
        for b in range(n):
            here = pl.ds(b * PRE_DEV, PRE_DEV)
            send_ref[b, pl.ds(0, PRE_DEV), :] = (dk_pre[here, :] * scale).astype(BF)
            send_ref[b, pl.ds(PRE_DEV, PRE_DEV), :] = dv_pre[here, :].astype(BF)
        first, rest = pl.ds(0, PRE_DEV), pl.ds(PRE_DEV, rows - PRE_DEV)
        d_ref[1, first, :] = jnp.zeros((PRE_DEV, HEAD_DIM), BF)
        d_ref[2, first, :] = jnp.zeros((PRE_DEV, HEAD_DIM), BF)
        d_ref[1, rest, :] = (dk_own[...] * scale).astype(BF)
        d_ref[2, rest, :] = dv_own[...].astype(BF)

    sol = rows - PRE_DEV
    flat = pl.BlockSpec((rows, HEAD_DIM), lambda h, m: (0, h))
    return call(
        body, "attention_backward", meta,
        (projected,) * 3 + tuple(prefix_kv) * 2 + (mixed, d_mixed, logs, d_out_matrix),
        attention_specs(rows, n)
        + [
            flat,
            flat,
            pl.BlockSpec((1, rows, 1), lambda h, m: (h, 0, 0)),
            pl.BlockSpec((n * share, HEAD_DIM), lambda h, m: (0, h)),
        ],
        [
            pl.BlockSpec((3, rows, HEAD_DIM), lambda h, m: (0, 0, h)),
            pl.BlockSpec((n, sent, HEAD_DIM), lambda h, m: (0, 0, h)),
        ],
        [
            jax.ShapeDtypeStruct((3, rows, width), BF),
            jax.ShapeDtypeStruct((n, sent, width), BF),
        ],
        grid=(heads,),
        scratch=[
            pltpu.VMEM((prefix, HEAD_DIM), BF),
            pltpu.VMEM((prefix, HEAD_DIM), BF),
            pltpu.VMEM((prefix, HEAD_DIM), FP),
            pltpu.VMEM((prefix, HEAD_DIM), FP),
            pltpu.VMEM((sol, HEAD_DIM), FP),
            pltpu.VMEM((sol, HEAD_DIM), FP),
        ],
    )


def adamw(weight, gradient, moment, variance, average, step_rate, decay_rate):
    moment = BETA_ONE * moment + (1.0 - BETA_ONE) * gradient
    variance = BETA_TWO * variance + (1.0 - BETA_TWO) * gradient * gradient
    corrected = moment / (1.0 - BETA_ONE**STEP)
    scaled_root = jnp.sqrt(variance / (1.0 - BETA_TWO**STEP)) + ADAM_EPS
    weight_new = weight - step_rate * corrected / scaled_root - step_rate * decay_rate * weight
    average = EMA_KEEP * average + (1.0 - EMA_KEEP) * weight_new
    return (moment, variance, weight_new, average)


def update_matrices(factor, groups, rates, steps):
    def spec(shape):
        if len(shape) == 3:
            return pl.BlockSpec((3, shape[1] // steps, shape[2]), lambda i: (0, i, 0))
        return pl.BlockSpec((shape[0] // steps, shape[1]), lambda i: (i, 0))

    flat = [array for group in groups for array in group]
    count = len(groups)
    shapes = [group[1].shape for group in groups]
    turned = [False, True, False, True]
    wide = [shape[0] // steps % 128 == 0 for shape in shapes]

    def body(factor_ref, *refs):
        scale = factor_ref[0]
        ins, outs, held = refs[: 5 * count], refs[5 * count : -1], refs[-1]
        for g in range(count):
            grad_ref, *old = ins[5 * g : 5 * g + 5]
            new = outs[4 * g : 4 * g + 4]
            if turned[g] and wide[g]:
                grad = jnp.transpose(grad_ref[...])
            elif turned[g]:
                size = shapes[g][0] // steps

                @pl.when(pl.program_id(0) == 0)
                def _():
                    held[...] = jnp.transpose(grad_ref[...])

                grad = held[pl.ds(pl.multiple_of(pl.program_id(0) * size, size), size), :]
            elif len(old[0].shape) < 3:
                grad = grad_ref[...]
            if len(old[0].shape) == 3:
                width = old[0].shape[2]
                for c in range(3):
                    grad = grad_ref[:, pl.ds(c * width, width)] * scale
                    results = adamw(
                        old[0][c], grad, old[1][c], old[2][c], old[3][c], rates[g], DECAY_MATRIX
                    )
                    for ref, value in zip(new, results):
                        ref[c] = value
            else:
                results = adamw(
                    old[0][...], grad * scale, old[1][...], old[2][...], old[3][...],
                    rates[g], DECAY_MATRIX,
                )
                for ref, value in zip(new, results):
                    ref[...] = value

    def gradient_spec(g):
        rows, columns = shapes[g]
        if g == 2:
            return pl.BlockSpec((rows // steps, columns), lambda i: (i + steps, 0))
        if wide[g]:
            return pl.BlockSpec((columns, rows // steps), lambda i: (0, i))
        return pl.BlockSpec((columns, rows), lambda i: (0, 0))

    results = [group[1] for group in groups for _ in range(4)]
    return pl.pallas_call(
        body,
        grid=(steps,),
        in_specs=[pl.BlockSpec(memory_space=pltpu.SMEM)]
        + [
            gradient_spec(g) if k == 0 and g > 0 else spec(a.shape)
            for g, group in enumerate(groups)
            for k, a in enumerate(group)
        ],
        out_specs=[spec(a.shape) for a in results],
        out_shape=[jax.ShapeDtypeStruct(a.shape, FP) for a in results],
        scratch_shapes=[pltpu.VMEM(shapes[1], FP)],
        compiler_params=PARAMS,
        name="update_matrices",
    )(factor, *flat)


class FeedScatter(Scatter):
    def __init__(self, ring, terms):
        self.terms = terms
        self.ring = ring
        self.left = ring.half
        self.send(*terms([ring.half], [[]], BF, True))

    def sums(self, order):
        j, n = self.left, self.ring.count
        rising, falling = self.fresh
        first = j == self.ring.half - 1
        return self.terms([j, n - j], [[(rising, 0)], [(falling, 1 if first else 0)]], BF)

    def advance(self, order):
        order.sums = self.sums(order)
        order.pin()
        self.send(*order.out.sums)

    def finish(self, order):
        while self.left:
            order.pin(self)
            self.advance(order)
        rising, falling = self.fresh
        return self.terms([0], [[(rising, 0), (falling, 0)]], FP)[0]


def pin(streams, *arrays):
    flat = [array for stream in streams for array in stream.fresh] + list(arrays)
    flat = list(lax.optimization_barrier(tuple(flat)))
    for stream in streams:
        stream.fresh = [flat.pop(0), flat.pop(0)]
        stream.arrive()
    return flat


class Taken:
    def __init__(self, arrays):
        self.__dict__["arrays"] = arrays

    def __getattr__(self, name):
        return self.arrays.pop(name)


class Order:
    def __init__(self, meta):
        self.meta = meta

    @property
    def out(self):
        return Taken(self.__dict__)

    def pin(self, *streams):
        arrays = self.__dict__
        names = sorted(arrays)
        leaves, tree = jax.tree.flatten([arrays[name] for name in names])
        arrays.update(zip(names, jax.tree.unflatten(tree, pin(streams, *leaves))))


def local(
    seq_count,
    head_count,
    tokens,
    cotangent,
    prefix_length,
    answer_lengths,
    inward,
    outward,
    expand,
    contract,
    norm_gains,
    moment_inward,
    moment_outward,
    moment_expand,
    moment_contract,
    moment_gains,
    variance_inward,
    variance_outward,
    variance_expand,
    variance_contract,
    variance_gains,
    average_inward,
    average_outward,
    average_expand,
    average_contract,
    average_gains,
):
    n, m = seq_count, head_count
    rows, model = tokens.shape
    share = model // n
    quarter = rows // m
    width = outward.shape[0]
    ring, team = Ring(n), Team(m)
    chips = team.chips

    device = lax.axis_index("seq")
    seq_table = []
    for s in range(n):
        place = ring.inverse[s]
        seq_table.append(
            [s] + [ring.order[(place + b) % n] for b in range(n)]
            + [(ring.inverse[t] - place) % n for t in range(n)]
        )
    seq_row = jnp.asarray(seq_table, jnp.int32)[device]
    head_row = jnp.asarray([team.quarters(h) for h in range(m)], jnp.int32)[lax.axis_index("head")]
    meta = jnp.concatenate(
        [seq_row[:1], prefix_length, answer_lengths, seq_row[1 : n + 1], head_row]
    ).astype(jnp.int32)
    blocks_of = seq_row[n + 1 :]
    places = META_IDS + n

    def flat_inward(array):
        return jnp.transpose(array, (1, 0, 2))

    def column_block(array, b):
        return array[:, b * share : (b + 1) * share]

    o = Order(meta)
    gain_row = norm_gains.astype(BF).reshape(-1, width)
    gain_row = jnp.pad(gain_row, ((0, 32 - gain_row.shape[0]), (0, 0)))
    gather_in = ring.gather(
        jnp.concatenate([flat_inward(inward).astype(BF).reshape(3 * share, width), gain_row], axis=0)
    )
    o.out_grad = mask_cotangent(meta, cotangent, n, m)
    o.up_shard = expand.astype(BF)
    o.down_shard = contract.astype(BF)
    o.out_shard = jnp.transpose(outward).astype(BF)
    o.pin(gather_in)
    gather_in.advance()
    o.pin(gather_in)
    gather_in.advance()
    o.pin(gather_in)
    gather_in.advance()
    o.pin(gather_in)
    in_blocks = gather_in.complete()
    gains = jnp.stack([block[3 * share : 3 * share + 2 * share // width] for block in in_blocks])
    gains = gains.reshape(n, 2, share).transpose(1, 0, 2).reshape(2, model).astype(FP)
    normed_prefix, _ = first_norm(o.meta, tokens, gains, PRE_DEV, n)
    o.kv_send = project_prefix(o.meta, normed_prefix, in_blocks, o.out.out_shard)
    o.pin()
    gather_kv = ring.gather(o.out.kv_send)
    gather_down = ring.gather(o.out.down_shard)
    o.normed_one, o.source = first_norm(o.meta, tokens, gains, rows, n)
    o.pin(gather_kv)
    gather_kv.advance()
    o.projected = project(o.meta, o.normed_one, in_blocks)
    o.pin(gather_kv, gather_down)
    gather_kv.advance()
    gather_down.advance()
    o.pin(gather_kv)
    gather_kv.advance()
    o.pin(gather_kv)
    kv_blocks = gather_kv.complete()
    gather_up = ring.gather(o.out.up_shard)

    o.mixed, o.logs = attention_forward(o.meta, o.projected, kv_blocks)
    o.pin(gather_down)
    gather_down.advance()
    out_rows = (2 * PRE_DEV, share)
    o.kept, o.away = rows_matmul(
        o.meta, "out_part", o.mixed, kv_blocks, m, True, out_rows, "nt"
    )
    o.pin(gather_up)
    gather_up.advance()
    o.got = team.cross(o.out.away)
    o.pin()
    o.arrived = team.send_sums(o.kept, o.got)
    o.pin(gather_down)
    kept, got, arrived = o.out.kept, o.out.got, o.out.arrived
    o.hidden, o.own = second_norm(
        o.meta, [kept, got] + arrived, o.source, gains, quarter, n
    )
    o.pin()
    o.parts = team.send_own(o.out.own)
    parts = o.out.parts
    o.pin(gather_up)
    gather_up.advance()
    gather_down.advance()
    o.parts = parts
    o.pin(gather_up)
    gather_up.advance()
    parts = team.send_half(o.out.parts)
    o.pin(gather_down)
    o.d_activation = feed_back(o.meta, o.out_grad, gather_down.complete())
    o.parts = parts
    o.pin(gather_up)
    o.normed_two, o.both = feed_up(
        o.meta, o.out.parts, gather_up.complete(), o.out.d_activation
    )

    def terms(blocks, received, dtype, cut=False):
        return feed_terms(
            o.meta, o.out_grad, o.normed_two, o.both, blocks, received, n, dtype, cut
        )

    sum_feed = FeedScatter(ring, terms)
    o.pin()
    o.kept, o.away = rows_matmul(
        o.meta, "up_back", o.both, gather_up.blocks, m, False, (0, None), "nt", 1
    )
    o.pin(sum_feed)
    o.got = team.cross(o.out.away)
    o.pin()
    kept, got = o.out.kept, o.out.got
    arrived = team.send_sums(kept, got)
    sum_feed.advance(o)
    o.terms = [kept, got] + arrived
    o.pin()
    o.d_hidden, o.own, o.gain_two = second_norm_back(
        o.meta, o.out.terms, o.hidden, o.out_grad, gains
    )
    o.pin()
    o.parts = team.send_own(o.out.own)

    o.kept, o.away = rows_matmul(
        o.meta, "down_part", o.both, gather_down.blocks, m, False, (0, None), "nn", 0
    )
    o.pin(sum_feed)
    parts = team.send_half(o.out.parts)
    kept, got = o.out.kept, team.cross(o.out.away)
    sum_feed.advance(o)
    o.parts, o.kept, o.got = parts, kept, got
    o.pin()

    o.d_attention, o.d_mixed, o.mixed_order = mixed_back(
        o.meta, o.out.parts, kv_blocks, o.mixed, 2 * PRE_DEV, n, m
    )
    o.d_out_matrix = jnp.einsum(
        "td,tn->dn", o.out.d_attention, o.out.mixed_order, preferred_element_type=FP
    ).astype(BF)
    o.pin()
    kept, got = o.out.kept, o.out.got
    arrived = team.send_sums(kept, got)
    o.d_parts, o.d_send = attention_backward(
        o.meta, o.projected, kv_blocks, o.out.mixed, o.out.d_mixed, o.out.logs,
        o.out.d_out_matrix,
    )
    o.terms = [kept, got] + arrived
    o.pin()

    def part_kv(b):
        return o.d_send[b].astype(FP)

    sum_kv = ring.scatter(part_kv(ring.half))
    result = o.hidden
    for term in o.out.terms:
        result = result + term[:quarter].astype(FP)
    o.own = result.astype(BF)
    o.pin()
    parts = team.send_own(o.out.own)
    o.pin(sum_kv)
    sum_kv.advance(part_kv, o)
    o.pin(sum_feed)
    o.sums = sum_feed.sums(o)
    o.parts = parts
    o.pin(sum_kv)
    sum_kv.advance(part_kv, o)
    parts = team.send_half(o.out.parts)
    o.parts = parts
    o.pin(sum_kv)
    sum_kv.advance(part_kv, o)
    sum_feed.send(*o.out.sums)
    o.layer_output = place_rows(o.meta, o.out.parts, n, m, BF)
    o.pin(sum_kv)

    red_kv_out = sum_kv.finish(part_kv, o)
    o.red_outward = red_kv_out[2 * PRE_DEV :]
    d_prefix = red_kv_out[: 2 * PRE_DEV].astype(BF).reshape(2, PRE_DEV, width)
    d_parts = lax.dynamic_update_slice(o.out.d_parts, d_prefix, (1, 0, 0))
    o.d_projected = jnp.concatenate([d_parts[0], d_parts[1], d_parts[2]], axis=1)
    o.out.d_send

    def part_inward(b):
        return jnp.einsum(
            "td,tn->dn", column_block(o.normed_one, b), o.d_projected, preferred_element_type=FP
        )

    o.far = part_inward(ring.half)
    o.pin()
    sum_inward = ring.scatter(o.out.far)
    o.kept, o.away = rows_matmul(
        o.meta, "in_back", o.d_projected, in_blocks, m, True, (0, 3 * share), "three"
    )
    o.pin(sum_inward)
    kept, got = o.out.kept, team.cross(o.out.away)
    sum_inward.advance(part_inward, o)
    o.kept, o.got = kept, got
    o.pin()
    kept, got = o.out.kept, o.out.got
    arrived = team.send_sums(kept, got)
    o.pin(sum_inward)
    sum_inward.advance(part_inward, o)
    o.terms = [kept, got] + arrived
    o.pin()
    o.own, o.gain_one = first_norm_back(
        o.meta, o.out.terms, o.source, o.d_hidden, gains, n
    )
    o.pin()
    parts = team.send_own(o.out.own)
    o.pin(sum_inward)
    sum_inward.advance(part_inward, o)
    o.parts = parts
    o.pin(sum_feed)
    o.parts = team.send_half(o.parts)
    o.red_feed = sum_feed.finish(o)
    o.out.both
    gain_parts = jnp.concatenate([o.out.gain_one, o.out.gain_two], axis=0).reshape(2, n, share)
    o.gain_parts = jnp.take(gain_parts, blocks_of, axis=1).reshape(2, model)
    red_feed, red_outward = o.out.red_feed, o.out.red_outward
    o.squares = jnp.sum(red_outward * red_outward) + jnp.sum(red_feed * red_feed)
    o.pin()
    o.input_grad = place_rows(o.meta, o.out.parts, n, m, FP)
    o.pin(sum_inward)
    red_inward = sum_inward.finish(part_inward, o)
    layer_output, input_grad, gain_parts = o.out.layer_output, o.out.input_grad, o.out.gain_parts

    squares = jnp.sum(red_inward * red_inward) + o.out.squares
    sums = jnp.concatenate([gain_parts, jnp.full((1, model), squares, FP)], axis=0)
    sums = total_of_all(sums, n, m)
    gain_sums = sums[:2]
    grad_norm = jnp.sqrt(sums[2, 0] + jnp.sum(gain_sums * gain_sums))
    factor = CLIP_NORM / jnp.maximum(grad_norm, CLIP_NORM)
    red_gains = lax.dynamic_slice(gain_sums, (0, device * share), (2, share))

    new = update_matrices(
        jnp.reshape(factor, (1,)),
        (
            (
                red_inward, flat_inward(inward), flat_inward(moment_inward),
                flat_inward(variance_inward), flat_inward(average_inward),
            ),
            (red_outward, outward, moment_outward, variance_outward, average_outward),
            (red_feed, expand, moment_expand, variance_expand, average_expand),
            (red_feed, contract, moment_contract, variance_contract, average_contract),
        ),
        (RATE_INWARD, RATE_OUTWARD, RATE_EXPAND, RATE_CONTRACT),
        4,
    )
    in_new = tuple(jnp.transpose(array, (1, 0, 2)) for array in new[:4])
    gain_new = adamw(
        norm_gains, red_gains * factor, moment_gains, variance_gains, average_gains, RATE_GAINS, 0.0
    )
    return (
        (layer_output, input_grad, jnp.reshape(grad_norm, (1,)))
        + in_new + tuple(new[4:]) + gain_new
    )


def solution(mesh):
    in_place = P("seq", None, "head")
    out_place = P("head", "seq")
    up_place = P("seq", "head")
    gain_place = P(None, "seq")
    weights = (in_place, out_place, up_place, out_place, gain_place)
    placed = (P("seq", None), P("seq", None), P(), P("seq")) + weights * 4
    results = (P("seq", None), P("seq", None), P())
    for place in weights:
        results += (place,) * 4
    return jax.shard_map(
        functools.partial(local, mesh.shape["seq"], mesh.shape["head"]),
        mesh=mesh,
        in_specs=placed,
        out_specs=results,
        check_vma=False,
    )
```

```python
import functools

import jax
import jax.numpy as jnp
from jax import lax
from jax.experimental import pallas as pl
from jax.experimental.pallas import tpu as pltpu
from jax.sharding import PartitionSpec as P

HEAD_DIM = 128
PRE_DEV = 256
SOL_DEV = 768
STEP = 10
BLOCK = 256

EPS_NORM = 1e-05
BETA_ONE = 0.9
BETA_TWO = 0.95
ADAM_EPS = 1e-08
EMA_KEEP = 0.7
CLIP_NORM = 1.0
DECAY_MATRIX = 0.1
RATE_INWARD = 0.05
RATE_OUTWARD = 0.15
RATE_EXPAND = 0.05
RATE_CONTRACT = 0.03
RATE_GAINS = 0.5

LOG2E = 1.4426950408889634
MASKED = -1e30
BF = jnp.bfloat16
FP = jnp.float32
VMEM_LIMIT = 56 * 1024 * 1024


def ring_order(count):
    depth = 4
    if count % depth or (count // depth) % 2:
        return list(range(count))
    width = count // depth
    order = [z * width for z in range(depth)]
    across = list(range(1, width))
    for z in reversed(range(depth)):
        order += [z * width + y for y in across]
        across = across[::-1]
    return order


class Ring:
    def __init__(self, count):
        self.count = count
        self.half = count // 2
        self.order = ring_order(count)
        self.up = [(self.order[i], self.order[(i + 1) % count]) for i in range(count)]
        self.down = [(b, a) for a, b in self.up]
        inverse = [0] * count
        for i, s in enumerate(self.order):
            inverse[s] = i
        self.inverse = inverse

    def gather(self, own):
        return Gather(self, own)

    def scatter(self, far):
        return Scatter(self, far)


class Gather:
    def __init__(self, ring, own):
        self.ring = ring
        self.blocks = [None] * ring.count
        self.blocks[0] = own
        self.fresh = [own, own]
        self.done = 0
        self.advance()

    def advance(self):
        ring = self.ring
        self.done += 1
        upper, lower = self.fresh
        if self.done == ring.half:
            mid = upper.shape[0] // 2
            upper, lower = upper[:mid], lower[mid:]
        self.fresh = [
            lax.ppermute(upper, "seq", ring.down),
            lax.ppermute(lower, "seq", ring.up),
        ]
        self.waiting = True

    def complete(self):
        while True:
            if self.waiting:
                pin([self])
            if self.done == self.ring.half:
                return self.blocks
            self.advance()

    def arrive(self):
        self.waiting = False
        j, n = self.done, self.ring.count
        if j == self.ring.half:
            self.blocks[j] = jnp.concatenate(self.fresh, axis=0)
        else:
            self.blocks[j], self.blocks[n - j] = self.fresh


class Scatter:
    def __init__(self, ring, far):
        self.ring = ring
        self.mid = far.shape[0] // 2
        self.left = ring.half
        self.send(far[: self.mid].astype(BF), far[self.mid :].astype(BF))

    def send(self, rising, falling):
        self.left -= 1
        self.fresh = [
            lax.ppermute(rising, "seq", self.ring.up),
            lax.ppermute(falling, "seq", self.ring.down),
        ]

    def arrive(self):
        pass

    def advance(self, part, order):
        j, mid = self.left, self.mid
        rising, falling = self.fresh
        upper, lower = part(j), part(self.ring.count - j)
        if j == self.ring.half - 1:
            upper = jnp.concatenate([upper[:mid] + rising.astype(FP), upper[mid:]], axis=0)
            lower = jnp.concatenate([lower[:mid], lower[mid:] + falling.astype(FP)], axis=0)
        else:
            upper = upper + rising.astype(FP)
            lower = lower + falling.astype(FP)
        order.upper, order.lower = upper.astype(BF), lower.astype(BF)
        order.pin()
        self.send(order.out.upper, order.out.lower)

    def finish(self, part, order):
        while self.left:
            order.pin(self)
            self.advance(part, order)
        return part(0) + self.fresh[0].astype(FP) + self.fresh[1].astype(FP)


class Team:
    def __init__(self, count):
        self.cores = 2 if count % 2 == 0 else 1
        self.chips = count // self.cores
        self.count = count
        self.core_flip = [(i, i ^ 1) for i in range(count)]

    def quarters(self, index):
        x, c = index // self.cores, index % self.cores
        cores = [c] + [1 - c] * (self.cores - 1)
        return [k * self.chips + (x + i) % self.chips for k in cores for i in range(self.chips)]

    def shift(self, k):
        chips, cores = self.chips, self.cores
        return [
            (x * cores + c, ((x + k) % chips) * cores + c) for x in range(chips) for c in range(cores)
        ]

    def cross(self, away):
        return lax.ppermute(away, "head", self.core_flip) if self.cores == 2 else None

    def send_sums(self, kept, got):
        size = kept.shape[0] // self.chips
        arrived = []
        for k in range(1, self.chips):
            spot = slice(k * size, (k + 1) * size)
            term = kept[spot].astype(FP)
            if got is not None:
                term = term + got[spot].astype(FP)
            arrived.append(lax.ppermute(term.astype(BF), "head", self.shift(k)))
        return arrived

    def send_own(self, own):
        return [own] + [lax.ppermute(own, "head", self.shift(-k)) for k in range(1, self.chips)]

    def send_half(self, parts):
        if self.cores == 1:
            return list(parts)
        half = jnp.concatenate(parts, axis=0) if self.chips > 1 else parts[0]
        return list(parts) + [lax.ppermute(half, "head", self.core_flip)]


def total_of_all(value, seq_count, head_count):
    for axis, count in (("head", head_count), ("seq", seq_count)):
        step = 1
        while step < count:
            value = value + lax.ppermute(value, axis, [(i, i ^ step) for i in range(count)])
            step *= 2
    return value


PARAMS = pltpu.CompilerParams(vmem_limit_bytes=VMEM_LIMIT)
ANYWHERE = pl.BlockSpec(memory_space=pl.ANY)
META_IDS = 3


def dot_nt(a, b):
    return lax.dot_general(a, b, (((1,), (1,)), ((), ())), preferred_element_type=FP)


def dot_nn(a, b):
    return lax.dot_general(a, b, (((1,), (0,)), ((), ())), preferred_element_type=FP)


def dot_tn(a, b):
    return lax.dot_general(a, b, (((0,), (0,)), ((), ())), preferred_element_type=FP)


def lanes(index, size):
    return pl.ds(pl.multiple_of(index * size, size), size)


def unit_of(values):
    center = values - jnp.mean(values, axis=-1, keepdims=True)
    inverse = lax.rsqrt(jnp.mean(center * center, axis=-1, keepdims=True) + EPS_NORM)
    return center * inverse, inverse


def norm_back(incoming, unit, inverse, gain_row):
    scaled = incoming * gain_row
    inner = (
        scaled
        - jnp.mean(scaled, axis=-1, keepdims=True)
        - unit * jnp.mean(scaled * unit, axis=-1, keepdims=True)
    )
    return inner * inverse, jnp.sum(incoming * unit, axis=0, keepdims=True)


def call(body, name, meta, inputs, in_specs, out_specs, out_shape, grid=(1,), scratch=()):
    return pl.pallas_call(
        body,
        grid_spec=pltpu.PrefetchScalarGridSpec(
            num_scalar_prefetch=1,
            grid=grid,
            in_specs=in_specs,
            out_specs=out_specs,
            scratch_shapes=list(scratch),
        ),
        out_shape=out_shape,
        compiler_params=PARAMS,
        cost_estimate=pl.CostEstimate(flops=1, bytes_accessed=1, transcendentals=0),
        name=name,
    )(meta, *inputs)


def first_norm(meta, tokens, gains, rows, n):
    model = tokens.shape[1]
    share = model // n

    def body(meta_ref, in_ref, gain_ref, norm_ref, source_ref, held):
        held[...], _ = unit_of(in_ref[...].astype(FP))
        for b in range(n):
            here = pl.ds(b * share, share)
            there = lanes(meta_ref[META_IDS + b], share)
            norm_ref[:, here] = (held[:, there] * gain_ref[0:1, here]).astype(BF)
            source_ref[:, here] = in_ref[:, there]

    tile = pl.BlockSpec((BLOCK, model), lambda i, m: (i, 0))
    return call(
        body, "first_norm", meta, (tokens, gains),
        [tile, pl.BlockSpec((2, model), lambda i, m: (0, 0))], [tile, tile],
        [jax.ShapeDtypeStruct((rows, model), BF), jax.ShapeDtypeStruct((rows, model), BF)],
        grid=(rows // BLOCK,),
        scratch=[pltpu.VMEM((BLOCK, model), FP)],
    )


def mask_cotangent(meta, cotangent, n, m):
    rows, model = cotangent.shape
    share, quarter = model // n, rows // m

    def body(meta_ref, in_ref, out_ref):
        spot = meta_ref[META_IDS + n + pl.program_id(0)] * quarter
        row = lax.broadcasted_iota(jnp.int32, (quarter, share), 0) + spot
        limit = jnp.where(
            row < PRE_DEV, meta_ref[1] - meta_ref[0] * PRE_DEV, meta_ref[2] + PRE_DEV
        )
        for b in range(n):
            piece = in_ref[:, lanes(meta_ref[META_IDS + b], share)]
            out_ref[:, pl.ds(b * share, share)] = jnp.where(row < limit, piece.astype(FP), 0).astype(BF)

    return call(
        body, "mask_cotangent", meta, (cotangent,),
        [pl.BlockSpec((quarter, model), lambda i, meta: (meta[META_IDS + n + i], 0))],
        pl.BlockSpec((quarter, model), lambda i, meta: (i, 0)),
        jax.ShapeDtypeStruct((rows, model), BF),
        grid=(m,),
    )


def place_rows(meta, pieces, n, m, dtype):
    quarter, model = pieces[0].shape
    share = model // n
    count = len(pieces)
    starts = [0]
    for piece in pieces:
        starts.append(starts[-1] + piece.shape[0] // quarter)

    def body(meta_ref, *refs):
        out_ref = refs[count]
        for k in range(count):

            @pl.when((pl.program_id(0) >= starts[k]) & (pl.program_id(0) < starts[k + 1]))
            def _():
                for b in range(n):
                    out_ref[:, lanes(meta_ref[META_IDS + b], share)] = refs[k][
                        :, pl.ds(b * share, share)
                    ].astype(dtype)

    def spec(k):
        last = starts[k + 1] - starts[k] - 1
        return pl.BlockSpec(
            (quarter, model), lambda i, meta: (jnp.clip(i - starts[k], 0, last), 0)
        )

    return call(
        body, "place_rows", meta, pieces, [spec(k) for k in range(count)],
        pl.BlockSpec((quarter, model), lambda i, meta: (meta[META_IDS + n + i], 0)),
        jax.ShapeDtypeStruct((quarter * m, model), dtype),
        grid=(m,),
    )


def project_prefix(meta, normed, weights, out_shard):
    n = len(weights)
    model = normed.shape[1]
    width = weights[0].shape[1]
    share = model // n

    def body(meta_ref, x_ref, shard_ref, *refs):
        blocks, (send_ref, held, sems) = refs[:n], refs[n:]

        def copy(b):
            return pltpu.make_async_copy(
                blocks[b].at[pl.ds(share, 2 * share), :], held.at[b], sems.at[b]
            )

        for b in range(n):
            copy(b).start()
        send_ref[pl.ds(2 * PRE_DEV, share), :] = shard_ref[...]
        totals = [None, None]
        for b in range(n):
            copy(b).wait()
            for c in range(2):
                term = dot_nn(
                    x_ref[:, pl.ds(b * share, share)], held[b, pl.ds(c * share, share), :]
                )
                totals[c] = term if b == 0 else totals[c] + term
        for c in range(2):
            send_ref[pl.ds(c * PRE_DEV, PRE_DEV), :] = totals[c].astype(BF)

    sent = 2 * PRE_DEV + share
    return call(
        body, "project_prefix", meta, (normed, out_shard, *weights),
        [
            pl.BlockSpec((PRE_DEV, model), lambda i, m: (0, 0)),
            pl.BlockSpec((share, width), lambda i, m: (0, 0)),
        ]
        + [ANYWHERE] * n,
        pl.BlockSpec((sent, width), lambda i, m: (0, 0)),
        jax.ShapeDtypeStruct((sent, width), BF),
        scratch=[pltpu.VMEM((n, 2 * share, width), BF), pltpu.SemaphoreType.DMA((n,))],
    )


def project(meta, normed, weights):
    n = len(weights)
    rows, model = normed.shape
    width = weights[0].shape[1]
    share = model // n

    def body(meta_ref, x_ref, *refs):
        blocks, (out_ref, held, sems) = refs[:n], refs[n:]
        part = pl.program_id(0)

        def copy(c, b):
            return pltpu.make_async_copy(
                blocks[b].at[pl.ds(pl.multiple_of(c * share, share), share), :],
                held.at[c, pl.ds(b * share, share), :],
                sems.at[c, b],
            )

        @pl.when(part == 0)
        def _():
            for c in range(3):
                for b in range(n):
                    copy(c, b).start()

        for b in range(n):
            copy(part, b).wait()
        out_ref[0] = dot_nn(x_ref[...], held[part]).astype(BF)

    return call(
        body, "project", meta, (normed, *weights),
        [pl.BlockSpec((rows, model), lambda c, m: (0, 0))] + [ANYWHERE] * n,
        pl.BlockSpec((1, rows, width), lambda c, m: (c, 0, 0)),
        jax.ShapeDtypeStruct((3, rows, width), BF),
        grid=(3,),
        scratch=[pltpu.VMEM((3, model, width), BF), pltpu.SemaphoreType.DMA((3, n))],
    )


def rows_matmul(meta, name, x, weights, m, placed, taken, form, layer=None):
    n = len(weights)
    rows, depth = x.shape[-2:]
    quarter = rows // m
    kept = quarter * (m // 2) if m % 2 == 0 else rows
    offset, size = taken
    width = weights[0].shape[1]
    held_rows = weights[0].shape[0] if size is None else size
    column = {"nn": width, "nt": held_rows}.get(form, held_rows // 3)
    group = max(1, min(n, 512 // column))
    tile = group * column
    steps = n // group

    def body(meta_ref, x_any, *refs):
        blocks, outs = refs[:n], refs[n:-4]
        x_held, held, x_sems, sems = refs[-4:]
        step = pl.program_id(0)

        def x_copy(i):
            spot = i * quarter
            if placed:
                spot = pl.multiple_of(meta_ref[META_IDS + n + i] * quarter, quarter)
            x_rows = x_any if layer is None else x_any.at[layer]
            return pltpu.make_async_copy(
                x_rows.at[pl.ds(spot, quarter), :],
                x_held.at[pl.ds(i * quarter, quarter), :],
                x_sems.at[i],
            )

        def copies(s, g):
            block = blocks[s * group + g]
            sem = sems.at[s, g]
            if form == "three":
                return [
                    pltpu.make_async_copy(
                        block.at[pl.ds(c * column, column), :],
                        held.at[s, pl.ds(g * column, column), pl.ds(c * width, width)],
                        sems.at[s, g * 3 + c],
                    )
                    for c in range(3)
                ]
            source = block if size is None else block.at[pl.ds(offset, size), :]
            if form == "nn":
                target = held.at[s, :, pl.ds(g * column, column)]
            else:
                target = held.at[s, pl.ds(g * column, column), :]
            return [pltpu.make_async_copy(source, target, sem)]

        @pl.when(step == 0)
        def _():
            for i in range(m):
                x_copy(i).start()
            for s in range(steps):
                for g in range(group):
                    for one in copies(s, g):
                        one.start()
            for i in range(m):
                x_copy(i).wait()

        for s in range(steps):

            @pl.when(step == s)
            def _():
                for g in range(group):
                    for one in copies(s, g):
                        one.wait()

        product = (dot_nn if form == "nn" else dot_nt)(x_held[...], held[step]).astype(BF)
        outs[0][...] = product[:kept]
        if kept < rows:
            outs[1][...] = product[kept:]

    if form == "nn":
        held_shape = (steps, depth, tile)
    else:
        held_shape = (steps, tile, depth)
    sizes = [kept] + ([rows - kept] if kept < rows else [])
    return call(
        body, name, meta, (x, *weights), [ANYWHERE] * (n + 1),
        [pl.BlockSpec((size_of, tile), lambda s, m: (0, s)) for size_of in sizes],
        [jax.ShapeDtypeStruct((size_of, n * column), BF) for size_of in sizes],
        grid=(steps,),
        scratch=[
            pltpu.VMEM((rows, depth), BF),
            pltpu.VMEM(held_shape, BF),
            pltpu.SemaphoreType.DMA((m,)),
            pltpu.SemaphoreType.DMA((steps, 3 * group if form == "three" else group)),
        ],
    )


def tile_of(width):
    return min(512, width)


def feed_back(meta, out_grad, weights):
    n = len(weights)
    rows, model = out_grad.shape
    width, share = weights[0].shape
    tile = tile_of(width)
    tiles = width // tile

    def body(meta_ref, x_ref, *refs):
        blocks, (out_ref, held, sems) = refs[:n], refs[n:]
        step = pl.program_id(0)

        def copy(t, b):
            return pltpu.make_async_copy(
                blocks[b].at[pl.ds(pl.multiple_of(t * tile, tile), tile), :],
                held.at[t, :, pl.ds(b * share, share)],
                sems.at[t, b],
            )

        @pl.when(step == 0)
        def _():
            for t in range(tiles):
                for b in range(n):
                    copy(t, b).start()

        for b in range(n):
            copy(step, b).wait()
        out_ref[...] = dot_nt(x_ref[...], held[step]).astype(BF)

    part = pl.BlockSpec((rows, tile), lambda t, m: (0, t))
    return call(
        body, "feed_back", meta, (out_grad, *weights),
        [pl.BlockSpec((rows, model), lambda t, m: (0, 0))] + [ANYWHERE] * n,
        part,
        jax.ShapeDtypeStruct((rows, width), BF),
        grid=(tiles,),
        scratch=[pltpu.VMEM((tiles, tile, model), BF), pltpu.SemaphoreType.DMA((tiles, n))],
    )


def feed_up(meta, pieces, weights, d_activation):
    n, count = len(weights), len(pieces)
    rows = sum(piece.shape[0] for piece in pieces)
    model = pieces[0].shape[1]
    width = weights[0].shape[1]
    share = model // n
    tile = tile_of(width)
    tiles = width // tile
    root = 0.7978845608028654
    step_rows = 512

    def body(meta_ref, *refs):
        parts, blocks, back_ref = refs[:count], refs[count : count + n], refs[count + n]
        x_out, both_ref, held, sems, x_sems = refs[count + n + 1 :]
        step = pl.program_id(0)

        def copy(t, b):
            return pltpu.make_async_copy(
                blocks[b].at[:, lanes(t, tile)],
                held.at[t, pl.ds(b * share, share), :],
                sems.at[t, b],
            )

        def x_copies():
            at, copies = 0, []
            for k in range(count):
                size = pieces[k].shape[0]
                copies.append(
                    pltpu.make_async_copy(parts[k], x_out.at[pl.ds(at, size), :], x_sems.at[k])
                )
                at += size
            return copies

        @pl.when(step == 0)
        def _():
            for one in x_copies():
                one.start()
            for t in range(tiles):
                for b in range(n):
                    copy(t, b).start()
            for one in x_copies():
                one.wait()

        for b in range(n):
            copy(step, b).wait()

        for i in range(rows // step_rows):
            spot = pl.ds(i * step_rows, step_rows)
            v = dot_nn(x_out[spot, :], held[step])
            square = v * v
            t = jnp.tanh(root * v * (1.0 + 0.044715 * square))
            half = 0.5 * (1.0 + t)
            both_ref[0, spot, :] = (v * half).astype(BF)
            slope = half + 0.5 * v * (1.0 - t * t) * (root * (1.0 + 3.0 * 0.044715 * square))
            both_ref[1, spot, :] = (back_ref[spot, :].astype(FP) * slope).astype(BF)

    return call(
        body, "feed_up", meta, (*pieces, *weights, d_activation),
        [ANYWHERE] * (count + n) + [pl.BlockSpec((rows, tile), lambda t, m: (0, t))],
        [
            pl.BlockSpec((rows, model), lambda t, m: (0, 0)),
            pl.BlockSpec((2, rows, tile), lambda t, m: (0, 0, t)),
        ],
        [
            jax.ShapeDtypeStruct((rows, model), BF),
            jax.ShapeDtypeStruct((2, rows, width), BF),
        ],
        grid=(tiles,),
        scratch=[
            pltpu.VMEM((tiles, model, tile), BF),
            pltpu.SemaphoreType.DMA((tiles, n)),
            pltpu.SemaphoreType.DMA((count,)),
        ],
    )


def feed_terms(meta, out_grad, normed, both, blocks, received, n, dtype, cut=False):
    rows, model = out_grad.shape
    width = both.shape[2]
    share = model // n
    count = len(blocks)
    flat = [(k, array, start) for k, sums in enumerate(received) for array, start in sums]

    def body(meta_ref, grad_ref, norm_ref, both_ref, *refs):
        arrived, outs = refs[: len(flat)], refs[len(flat) :]
        matrix, block = pl.program_id(0), pl.program_id(1)
        for k in range(count):
            for which, left in ((0, grad_ref), (1, norm_ref)):

                @pl.when((matrix == which) & (block == k))
                def _():
                    term = dot_tn(left[...], both_ref[0])
                    for (at, array, start), ref in zip(flat, arrived):
                        if at == k and start <= which < start + array.shape[0] // share:
                            term = term + ref[...].astype(FP)
                    outs[which if cut else k][...] = term.astype(dtype)

    def chosen(k):
        b = blocks[0]
        for i in range(1, count):
            b = jnp.where(k == i, blocks[i], b)
        return b

    def received_spec(array, start):
        last = array.shape[0] // share - 1
        return pl.BlockSpec((share, width), lambda t, k, m: (jnp.clip(t - start, 0, last), 0))

    column = pl.BlockSpec((rows, share), lambda t, k, m: (0, chosen(k)))
    out = call(
        body, "feed_terms", meta, (out_grad, normed, both, *[array for _, array, _ in flat]),
        [column, column, pl.BlockSpec((1, rows, width), lambda t, k, m: (t, 0, 0))]
        + [received_spec(array, start) for _, array, start in flat],
        [pl.BlockSpec((share, width), lambda t, k, m: (0 if cut else t, 0))] * (2 if cut else count),
        [jax.ShapeDtypeStruct(((1 if cut else 2) * share, width), dtype)] * (2 if cut else count),
        grid=(2, count),
    )
    return out


def mixed_back(meta, pieces, weights, mixed, offset, n, m):
    count = len(pieces)
    quarter, model = pieces[0].shape
    share = model // n
    rows, width = mixed.shape

    def body(meta_ref, *refs):
        parts, blocks, mixed_ref = refs[:count], refs[count : count + n], refs[count + n]
        x_out, d_ref, mixed_out, held, sems, x_sems = refs[count + n + 1 :]
        step = pl.program_id(0)

        def copy(b):
            return pltpu.make_async_copy(
                blocks[b].at[pl.ds(offset, share), :],
                held.at[pl.ds(b * share, share), :],
                sems.at[b],
            )

        def x_copies():
            at, copies = 0, []
            for k in range(count):
                size = pieces[k].shape[0]
                copies.append(
                    pltpu.make_async_copy(parts[k], x_out.at[pl.ds(at, size), :], x_sems.at[k])
                )
                at += size
            return copies

        @pl.when(step == 0)
        def _():
            for one in x_copies() + [copy(b) for b in range(n)]:
                one.start()
            for one in x_copies() + [copy(b) for b in range(n)]:
                one.wait()

        spot = pl.ds(pl.multiple_of(step * quarter, quarter), quarter)
        d_ref[...] = dot_nn(x_out[spot, :], held[...]).astype(BF)
        mixed_out[...] = mixed_ref[...]

    placed = pl.BlockSpec((quarter, width), lambda i, meta: (meta[META_IDS + n + i], 0))
    return call(
        body, "mixed_back", meta, (*pieces, *weights, mixed),
        [ANYWHERE] * (count + n) + [placed],
        [
            pl.BlockSpec((rows, model), lambda i, meta: (0, 0)),
            placed,
            pl.BlockSpec((quarter, width), lambda i, meta: (i, 0)),
        ],
        [
            jax.ShapeDtypeStruct((rows, model), BF),
            jax.ShapeDtypeStruct((rows, width), BF),
            jax.ShapeDtypeStruct((rows, width), BF),
        ],
        grid=(m,),
        scratch=[
            pltpu.VMEM((model, width), BF),
            pltpu.SemaphoreType.DMA((n,)),
            pltpu.SemaphoreType.DMA((count,)),
        ],
    )


def own_quarter(quarter, model, step):
    steps = quarter // step
    plain = pl.BlockSpec((step, model), lambda i, meta: (i, 0))
    whole = pl.BlockSpec((2, model), lambda i, meta: (0, 0))

    def placed(n):
        return pl.BlockSpec(
            (step, model), lambda i, meta: (meta[META_IDS + n] * steps + i, 0)
        )

    return steps, plain, whole, placed


def second_norm(meta, terms, source, gains, quarter, n):
    model = source.shape[1]
    steps, plain, whole, placed = own_quarter(quarter, model, min(64, quarter))
    count = len(terms)

    def body(meta_ref, *refs):
        source_ref, gain_ref, hidden_ref, norm_ref = refs[count:]
        hidden = refs[0][...].astype(FP)
        for k in range(1, count):
            hidden = hidden + refs[k][...].astype(FP)
        hidden = source_ref[...].astype(FP) + hidden
        hidden_ref[...] = hidden
        norm_ref[...] = (unit_of(hidden)[0] * gain_ref[1:2, :]).astype(BF)

    return call(
        body, "second_norm", meta, (*terms, source, gains),
        [plain] * count + [placed(n), whole], [plain, plain],
        [jax.ShapeDtypeStruct((quarter, model), FP), jax.ShapeDtypeStruct((quarter, model), BF)],
        grid=(steps,),
    )


def second_norm_back(meta, terms, hidden, out_grad, gains):
    quarter, model = hidden.shape
    steps, plain, whole, _ = own_quarter(quarter, model, min(64, quarter))
    count = len(terms)

    def body(meta_ref, *refs):
        hidden_ref, grad_ref, gain_ref, d_ref, low_ref, dg_ref = refs[count:]
        incoming = refs[0][...].astype(FP)
        for k in range(1, count):
            incoming = incoming + refs[k][...].astype(FP)
        unit, inverse = unit_of(hidden_ref[...])
        d_norm, d_gain = norm_back(incoming, unit, inverse, gain_ref[1:2, :])
        d_hidden = grad_ref[...].astype(FP) + d_norm
        d_ref[...] = d_hidden
        low_ref[...] = d_hidden.astype(BF)

        @pl.when(pl.program_id(0) == 0)
        def _():
            dg_ref[...] = d_gain

        @pl.when(pl.program_id(0) > 0)
        def _():
            dg_ref[...] += d_gain

    return call(
        body, "second_norm_back", meta, (*terms, hidden, out_grad, gains),
        [plain] * (count + 2) + [whole],
        [plain, plain, pl.BlockSpec((1, model), lambda i, m: (0, 0))],
        [
            jax.ShapeDtypeStruct((quarter, model), FP),
            jax.ShapeDtypeStruct((quarter, model), BF),
            jax.ShapeDtypeStruct((1, model), FP),
        ],
        grid=(steps,),
    )


def first_norm_back(meta, terms, source, d_hidden, gains, n):
    quarter, model = d_hidden.shape
    steps, plain, whole, placed = own_quarter(quarter, model, min(64, quarter))
    count = len(terms)

    def body(meta_ref, *refs):
        source_ref, hidden_ref, gain_ref, low_ref, dg_ref = refs[count:]
        incoming = refs[0][...].astype(FP)
        for k in range(1, count):
            incoming = incoming + refs[k][...].astype(FP)
        unit, inverse = unit_of(source_ref[...].astype(FP))
        d_norm, d_gain = norm_back(incoming, unit, inverse, gain_ref[0:1, :])
        low_ref[...] = (hidden_ref[...] + d_norm).astype(BF)

        @pl.when(pl.program_id(0) == 0)
        def _():
            dg_ref[...] = d_gain

        @pl.when(pl.program_id(0) > 0)
        def _():
            dg_ref[...] += d_gain

    return call(
        body, "first_norm_back", meta, (*terms, source, d_hidden, gains),
        [plain] * count + [placed(n), plain, whole],
        [plain, pl.BlockSpec((1, model), lambda i, m: (0, 0))],
        [jax.ShapeDtypeStruct((quarter, model), BF), jax.ShapeDtypeStruct((1, model), FP)],
        grid=(steps,),
    )


def prefix_places(meta_ref, n):
    spot = lax.broadcasted_iota(jnp.int32, (1, PRE_DEV), 1)
    return jnp.concatenate([spot + meta_ref[META_IDS + b] * PRE_DEV for b in range(n)], axis=1)


def masked_scores(meta_ref, q_ref, k_ref, kp_ref, places, block):
    limit_prefix = meta_ref[1]
    limit_answer = meta_ref[2]
    query = q_ref[0, pl.ds(block * BLOCK, BLOCK), :]
    score_pre = dot_nt(query, kp_ref[...])
    if block < PRE_DEV // BLOCK:
        row = lax.broadcasted_iota(jnp.int32, (BLOCK, 1), 0) + block * BLOCK
        reach = jnp.minimum(meta_ref[0] * PRE_DEV + row + 1, limit_prefix)
        return query, jnp.where(places < reach, score_pre, MASKED), None
    score_pre = jnp.where(places < limit_prefix, score_pre, MASKED)
    solution_row = block * BLOCK - PRE_DEV
    width = solution_row + BLOCK
    score_own = dot_nt(query, k_ref[0, pl.ds(PRE_DEV, width), :])
    row = lax.broadcasted_iota(jnp.int32, (BLOCK, 1), 0) + solution_row
    reach = jnp.minimum(row + 1, limit_answer)
    column = lax.broadcasted_iota(jnp.int32, (1, width), 1)
    return query, score_pre, jnp.where(column < reach, score_own, MASKED)


def attention_specs(rows, n):
    part = lambda c: pl.BlockSpec((1, rows, HEAD_DIM), lambda h, m: (c, 0, h))
    pre = lambda c: pl.BlockSpec((PRE_DEV, HEAD_DIM), lambda h, m: (c, h))
    return [part(0), part(1), part(2)] + [pre(0)] * n + [pre(1)] * n


def attention_forward(meta, projected, prefix_kv):
    _, rows, width = projected.shape
    heads = width // HEAD_DIM
    n = len(prefix_kv)
    prefix = n * PRE_DEV
    scale = HEAD_DIM ** (-0.5) * LOG2E

    def body(meta_ref, q_ref, k_ref, v_ref, *refs):
        keys, values, (out_ref, log_ref, kp_ref, vp_ref) = refs[:n], refs[n : 2 * n], refs[2 * n :]
        for b in range(n):
            kp_ref[pl.ds(b * PRE_DEV, PRE_DEV), :] = keys[b][...]
            vp_ref[pl.ds(b * PRE_DEV, PRE_DEV), :] = values[b][...]
        places = prefix_places(meta_ref, n)
        for block in range(rows // BLOCK):
            _, score_pre, score_own = masked_scores(meta_ref, q_ref, k_ref, kp_ref, places, block)
            top = jnp.max(score_pre, axis=-1, keepdims=True)
            if score_own is not None:
                top = jnp.maximum(top, jnp.max(score_own, axis=-1, keepdims=True))
            e_pre = jnp.exp2((score_pre - top) * scale)
            total = jnp.sum(e_pre, axis=-1, keepdims=True)
            out = dot_nn(e_pre.astype(BF), vp_ref[...])
            if score_own is not None:
                e_own = jnp.exp2((score_own - top) * scale)
                total = total + jnp.sum(e_own, axis=-1, keepdims=True)
                out = out + dot_nn(
                    e_own.astype(BF), v_ref[0, pl.ds(PRE_DEV, score_own.shape[1]), :]
                )
            out_ref[pl.ds(block * BLOCK, BLOCK), :] = (out / total).astype(BF)
            log_ref[0, pl.ds(block * BLOCK, BLOCK), :] = top * scale + jnp.log2(total)

    return call(
        body, "attention_forward", meta, (projected,) * 3 + tuple(prefix_kv) * 2,
        attention_specs(rows, n),
        [
            pl.BlockSpec((rows, HEAD_DIM), lambda h, m: (0, h)),
            pl.BlockSpec((1, rows, 1), lambda h, m: (h, 0, 0)),
        ],
        [
            jax.ShapeDtypeStruct((rows, heads * HEAD_DIM), BF),
            jax.ShapeDtypeStruct((heads, rows, 1), FP),
        ],
        grid=(heads,),
        scratch=[pltpu.VMEM((prefix, HEAD_DIM), BF), pltpu.VMEM((prefix, HEAD_DIM), BF)],
    )


def attention_backward(meta, projected, prefix_kv, mixed, d_mixed, logs, d_out_matrix):
    _, rows, width = projected.shape
    heads = width // HEAD_DIM
    n = len(prefix_kv)
    prefix = n * PRE_DEV
    share = d_out_matrix.shape[0] // n
    scale = HEAD_DIM ** (-0.5)
    sent = 2 * PRE_DEV + share

    def body(meta_ref, q_ref, k_ref, v_ref, *refs):
        keys, values = refs[:n], refs[n : 2 * n]
        o_ref, do_ref, log_ref, matrix_ref, d_ref, send_ref = refs[2 * n : 2 * n + 6]
        kp_ref, vp_ref, dk_pre, dv_pre, dk_own, dv_own = refs[2 * n + 6 :]
        for b in range(n):
            kp_ref[pl.ds(b * PRE_DEV, PRE_DEV), :] = keys[b][...]
            vp_ref[pl.ds(b * PRE_DEV, PRE_DEV), :] = values[b][...]
            send_ref[b, pl.ds(2 * PRE_DEV, share), :] = matrix_ref[pl.ds(b * share, share), :]
        places = prefix_places(meta_ref, n)
        dk_own[...] = jnp.zeros_like(dk_own)
        dv_own[...] = jnp.zeros_like(dv_own)
        for block in range(rows // BLOCK):
            spot = pl.ds(block * BLOCK, BLOCK)
            query, score_pre, score_own = masked_scores(
                meta_ref, q_ref, k_ref, kp_ref, places, block
            )
            d_out = do_ref[spot, :]
            log = log_ref[0, spot, :]
            inner = jnp.sum(d_out.astype(FP) * o_ref[spot, :].astype(FP), axis=-1, keepdims=True)
            p = jnp.exp2(score_pre * (scale * LOG2E) - log)
            ds = (p * (dot_nt(d_out, vp_ref[...]) - inner)).astype(BF)
            p = p.astype(BF)
            dq = dot_nn(ds, kp_ref[...])
            dk_term = dot_tn(ds, query)
            dv_term = dot_tn(p, d_out)
            if block == 0:
                dk_pre[...] = dk_term
                dv_pre[...] = dv_term
            else:
                dk_pre[...] += dk_term
                dv_pre[...] += dv_term
            if score_own is not None:
                near = pl.ds(PRE_DEV, score_own.shape[1])
                p = jnp.exp2(score_own * (scale * LOG2E) - log)
                ds = (p * (dot_nt(d_out, v_ref[0, near, :]) - inner)).astype(BF)
                p = p.astype(BF)
                dq = dq + dot_nn(ds, k_ref[0, near, :])
                own = pl.ds(0, score_own.shape[1])
                dk_own[own, :] += dot_tn(ds, query)
                dv_own[own, :] += dot_tn(p, d_out)
            d_ref[0, spot, :] = (dq * scale).astype(BF)
        for b in range(n):
            here = pl.ds(b * PRE_DEV, PRE_DEV)
            send_ref[b, pl.ds(0, PRE_DEV), :] = (dk_pre[here, :] * scale).astype(BF)
            send_ref[b, pl.ds(PRE_DEV, PRE_DEV), :] = dv_pre[here, :].astype(BF)
        first, rest = pl.ds(0, PRE_DEV), pl.ds(PRE_DEV, rows - PRE_DEV)
        d_ref[1, first, :] = jnp.zeros((PRE_DEV, HEAD_DIM), BF)
        d_ref[2, first, :] = jnp.zeros((PRE_DEV, HEAD_DIM), BF)
        d_ref[1, rest, :] = (dk_own[...] * scale).astype(BF)
        d_ref[2, rest, :] = dv_own[...].astype(BF)

    sol = rows - PRE_DEV
    flat = pl.BlockSpec((rows, HEAD_DIM), lambda h, m: (0, h))
    return call(
        body, "attention_backward", meta,
        (projected,) * 3 + tuple(prefix_kv) * 2 + (mixed, d_mixed, logs, d_out_matrix),
        attention_specs(rows, n)
        + [
            flat,
            flat,
            pl.BlockSpec((1, rows, 1), lambda h, m: (h, 0, 0)),
            pl.BlockSpec((n * share, HEAD_DIM), lambda h, m: (0, h)),
        ],
        [
            pl.BlockSpec((3, rows, HEAD_DIM), lambda h, m: (0, 0, h)),
            pl.BlockSpec((n, sent, HEAD_DIM), lambda h, m: (0, 0, h)),
        ],
        [
            jax.ShapeDtypeStruct((3, rows, width), BF),
            jax.ShapeDtypeStruct((n, sent, width), BF),
        ],
        grid=(heads,),
        scratch=[
            pltpu.VMEM((prefix, HEAD_DIM), BF),
            pltpu.VMEM((prefix, HEAD_DIM), BF),
            pltpu.VMEM((prefix, HEAD_DIM), FP),
            pltpu.VMEM((prefix, HEAD_DIM), FP),
            pltpu.VMEM((sol, HEAD_DIM), FP),
            pltpu.VMEM((sol, HEAD_DIM), FP),
        ],
    )


def adamw(weight, gradient, moment, variance, average, step_rate, decay_rate):
    moment = BETA_ONE * moment + (1.0 - BETA_ONE) * gradient
    variance = BETA_TWO * variance + (1.0 - BETA_TWO) * gradient * gradient
    corrected = moment / (1.0 - BETA_ONE**STEP)
    scaled_root = jnp.sqrt(variance / (1.0 - BETA_TWO**STEP)) + ADAM_EPS
    weight_new = weight - step_rate * corrected / scaled_root - step_rate * decay_rate * weight
    average = EMA_KEEP * average + (1.0 - EMA_KEEP) * weight_new
    return (moment, variance, weight_new, average)


def update_matrices(factor, groups, rates, steps):
    def spec(shape):
        if len(shape) == 3:
            return pl.BlockSpec((3, shape[1] // steps, shape[2]), lambda i: (0, i, 0))
        return pl.BlockSpec((shape[0] // steps, shape[1]), lambda i: (i, 0))

    flat = [array for group in groups for array in group]
    count = len(groups)
    shapes = [group[1].shape for group in groups]
    turned = [False, True, False, True]
    wide = [shape[0] // steps % 128 == 0 for shape in shapes]

    def body(factor_ref, *refs):
        scale = factor_ref[0]
        ins, outs, held = refs[: 5 * count], refs[5 * count : -1], refs[-1]
        for g in range(count):
            grad_ref, *old = ins[5 * g : 5 * g + 5]
            new = outs[4 * g : 4 * g + 4]
            if turned[g] and wide[g]:
                grad = jnp.transpose(grad_ref[...])
            elif turned[g]:
                size = shapes[g][0] // steps

                @pl.when(pl.program_id(0) == 0)
                def _():
                    held[...] = jnp.transpose(grad_ref[...])

                grad = held[pl.ds(pl.multiple_of(pl.program_id(0) * size, size), size), :]
            elif len(old[0].shape) < 3:
                grad = grad_ref[...]
            if len(old[0].shape) == 3:
                width = old[0].shape[2]
                for c in range(3):
                    grad = grad_ref[:, pl.ds(c * width, width)] * scale
                    results = adamw(
                        old[0][c], grad, old[1][c], old[2][c], old[3][c], rates[g], DECAY_MATRIX
                    )
                    for ref, value in zip(new, results):
                        ref[c] = value
            else:
                results = adamw(
                    old[0][...], grad * scale, old[1][...], old[2][...], old[3][...],
                    rates[g], DECAY_MATRIX,
                )
                for ref, value in zip(new, results):
                    ref[...] = value

    def gradient_spec(g):
        rows, columns = shapes[g]
        if g == 2:
            return pl.BlockSpec((rows // steps, columns), lambda i: (i + steps, 0))
        if wide[g]:
            return pl.BlockSpec((columns, rows // steps), lambda i: (0, i))
        return pl.BlockSpec((columns, rows), lambda i: (0, 0))

    results = [group[1] for group in groups for _ in range(4)]
    return pl.pallas_call(
        body,
        grid=(steps,),
        in_specs=[pl.BlockSpec(memory_space=pltpu.SMEM)]
        + [
            gradient_spec(g) if k == 0 and g > 0 else spec(a.shape)
            for g, group in enumerate(groups)
            for k, a in enumerate(group)
        ],
        out_specs=[spec(a.shape) for a in results],
        out_shape=[jax.ShapeDtypeStruct(a.shape, FP) for a in results],
        scratch_shapes=[pltpu.VMEM(shapes[1], FP)],
        compiler_params=PARAMS,
        name="update_matrices",
    )(factor, *flat)


class FeedScatter(Scatter):
    def __init__(self, ring, terms):
        self.terms = terms
        self.ring = ring
        self.left = ring.half
        self.send(*terms([ring.half], [[]], BF, True))

    def sums(self, order):
        j, n = self.left, self.ring.count
        rising, falling = self.fresh
        first = j == self.ring.half - 1
        return self.terms([j, n - j], [[(rising, 0)], [(falling, 1 if first else 0)]], BF)

    def raw(self):
        return self.terms([self.left, self.ring.count - self.left], [[], []], BF)

    def added(self, raw):
        return [
            (term.astype(FP) + got.astype(FP)).astype(BF) for term, got in zip(raw, self.fresh)
        ]

    def advance(self, order):
        order.sums = self.sums(order)
        order.pin()
        self.send(*order.out.sums)

    def finish(self, order):
        while self.left:
            order.pin(self)
            self.advance(order)
        rising, falling = self.fresh
        return self.terms([0], [[(rising, 0), (falling, 0)]], FP)[0]


def pin(streams, *arrays):
    flat = [array for stream in streams for array in stream.fresh] + list(arrays)
    flat = list(lax.optimization_barrier(tuple(flat)))
    for stream in streams:
        stream.fresh = [flat.pop(0), flat.pop(0)]
        stream.arrive()
    return flat


class Taken:
    def __init__(self, arrays):
        self.__dict__["arrays"] = arrays

    def __getattr__(self, name):
        return self.arrays.pop(name)


class Order:
    def __init__(self, meta):
        self.meta = meta

    @property
    def out(self):
        return Taken(self.__dict__)

    def pin(self, *streams):
        arrays = self.__dict__
        names = sorted(arrays)
        leaves, tree = jax.tree.flatten([arrays[name] for name in names])
        arrays.update(zip(names, jax.tree.unflatten(tree, pin(streams, *leaves))))


def local(
    seq_count,
    head_count,
    tokens,
    cotangent,
    prefix_length,
    answer_lengths,
    inward,
    outward,
    expand,
    contract,
    norm_gains,
    moment_inward,
    moment_outward,
    moment_expand,
    moment_contract,
    moment_gains,
    variance_inward,
    variance_outward,
    variance_expand,
    variance_contract,
    variance_gains,
    average_inward,
    average_outward,
    average_expand,
    average_contract,
    average_gains,
):
    n, m = seq_count, head_count
    rows, model = tokens.shape
    share = model // n
    quarter = rows // m
    width = outward.shape[0]
    ring, team = Ring(n), Team(m)
    chips = team.chips

    device = lax.axis_index("seq")
    seq_table = []
    for s in range(n):
        place = ring.inverse[s]
        seq_table.append(
            [s] + [ring.order[(place + b) % n] for b in range(n)]
            + [(ring.inverse[t] - place) % n for t in range(n)]
        )
    seq_row = jnp.asarray(seq_table, jnp.int32)[device]
    head_row = jnp.asarray([team.quarters(h) for h in range(m)], jnp.int32)[lax.axis_index("head")]
    meta = jnp.concatenate(
        [seq_row[:1], prefix_length, answer_lengths, seq_row[1 : n + 1], head_row]
    ).astype(jnp.int32)
    blocks_of = seq_row[n + 1 :]
    places = META_IDS + n

    def flat_inward(array):
        return jnp.transpose(array, (1, 0, 2))

    def column_block(array, b):
        return array[:, b * share : (b + 1) * share]

    o = Order(meta)
    gain_row = norm_gains.astype(BF).reshape(-1, width)
    gain_row = jnp.pad(gain_row, ((0, 32 - gain_row.shape[0]), (0, 0)))
    gather_in = ring.gather(
        jnp.concatenate([flat_inward(inward).astype(BF).reshape(3 * share, width), gain_row], axis=0)
    )
    o.out_grad = mask_cotangent(meta, cotangent, n, m)
    o.up_shard = expand.astype(BF)
    o.down_shard = contract.astype(BF)
    o.out_shard = jnp.transpose(outward).astype(BF)
    o.pin(gather_in)
    gather_in.advance()
    o.pin(gather_in)
    gather_in.advance()
    o.pin(gather_in)
    gather_in.advance()
    o.pin(gather_in)
    in_blocks = gather_in.complete()
    gains = jnp.stack([block[3 * share : 3 * share + 2 * share // width] for block in in_blocks])
    gains = gains.reshape(n, 2, share).transpose(1, 0, 2).reshape(2, model).astype(FP)
    normed_prefix, _ = first_norm(o.meta, tokens, gains, PRE_DEV, n)
    o.kv_send = project_prefix(o.meta, normed_prefix, in_blocks, o.out.out_shard)
    o.pin()
    gather_kv = ring.gather(o.out.kv_send)
    gather_down = ring.gather(o.out.down_shard)
    o.normed_one, o.source = first_norm(o.meta, tokens, gains, rows, n)
    o.pin(gather_kv)
    gather_kv.advance()
    o.projected = project(o.meta, o.normed_one, in_blocks)
    o.pin(gather_kv, gather_down)
    gather_kv.advance()
    gather_down.advance()
    o.pin(gather_kv)
    gather_kv.advance()
    o.pin(gather_kv)
    kv_blocks = gather_kv.complete()
    gather_up = ring.gather(o.out.up_shard)

    o.mixed, o.logs = attention_forward(o.meta, o.projected, kv_blocks)
    o.pin(gather_down)
    gather_down.advance()
    out_rows = (2 * PRE_DEV, share)
    o.kept, o.away = rows_matmul(
        o.meta, "out_part", o.mixed, kv_blocks, m, True, out_rows, "nt"
    )
    o.pin(gather_up)
    gather_up.advance()
    o.got = team.cross(o.out.away)
    o.pin()
    o.arrived = team.send_sums(o.kept, o.got)
    o.pin(gather_down)
    kept, got, arrived = o.out.kept, o.out.got, o.out.arrived
    o.hidden, o.own = second_norm(
        o.meta, [kept, got] + arrived, o.source, gains, quarter, n
    )
    o.pin()
    o.parts = team.send_own(o.out.own)
    parts = o.out.parts
    o.pin(gather_up)
    gather_up.advance()
    gather_down.advance()
    o.parts = parts
    o.pin(gather_up)
    gather_up.advance()
    parts = team.send_half(o.out.parts)
    o.pin(gather_down)
    o.d_activation = feed_back(o.meta, o.out_grad, gather_down.complete())
    o.parts = parts
    o.pin(gather_up)
    o.normed_two, o.both = feed_up(
        o.meta, o.out.parts, gather_up.complete(), o.out.d_activation
    )

    def terms(blocks, received, dtype, cut=False):
        return feed_terms(
            o.meta, o.out_grad, o.normed_two, o.both, blocks, received, n, dtype, cut
        )

    sum_feed = FeedScatter(ring, terms)
    o.pin()
    o.kept, o.away = rows_matmul(
        o.meta, "up_back", o.both, gather_up.blocks, m, False, (0, None), "nt", 1
    )
    o.pin(sum_feed)
    o.got = team.cross(o.out.away)
    o.pin()
    kept, got = o.out.kept, o.out.got
    arrived = team.send_sums(kept, got)
    sum_feed.advance(o)
    o.terms = [kept, got] + arrived
    o.pin()
    o.d_hidden, o.own, o.gain_two = second_norm_back(
        o.meta, o.out.terms, o.hidden, o.out_grad, gains
    )
    o.pin()
    o.parts = team.send_own(o.out.own)

    o.kept, o.away = rows_matmul(
        o.meta, "down_part", o.both, gather_down.blocks, m, False, (0, None), "nn", 0
    )
    o.raw = sum_feed.raw()
    o.pin(sum_feed)
    parts = team.send_half(o.out.parts)
    kept, got = o.out.kept, team.cross(o.out.away)
    o.sums = sum_feed.added(o.out.raw)
    o.pin()
    sum_feed.send(*o.out.sums)
    o.parts, o.kept, o.got = parts, kept, got
    o.pin()

    o.d_attention, o.d_mixed, o.mixed_order = mixed_back(
        o.meta, o.out.parts, kv_blocks, o.mixed, 2 * PRE_DEV, n, m
    )
    o.d_out_matrix = jnp.einsum(
        "td,tn->dn", o.out.d_attention, o.out.mixed_order, preferred_element_type=FP
    ).astype(BF)
    o.pin()
    kept, got = o.out.kept, o.out.got
    arrived = team.send_sums(kept, got)
    o.d_parts, o.d_send = attention_backward(
        o.meta, o.projected, kv_blocks, o.out.mixed, o.out.d_mixed, o.out.logs,
        o.out.d_out_matrix,
    )
    o.terms = [kept, got] + arrived
    o.pin(sum_feed)

    def part_kv(b):
        return o.d_send[b].astype(FP)

    sum_kv = ring.scatter(part_kv(ring.half))
    result = o.hidden
    for term in o.out.terms:
        result = result + term[:quarter].astype(FP)
    o.own = result.astype(BF)
    o.pin()
    parts = team.send_own(o.out.own)
    o.pin(sum_kv)
    sum_kv.advance(part_kv, o)
    o.pin(sum_feed)
    o.sums = sum_feed.sums(o)
    o.parts = parts
    o.pin(sum_kv)
    sum_kv.advance(part_kv, o)
    parts = team.send_half(o.out.parts)
    o.parts = parts
    o.pin(sum_kv)
    sum_kv.advance(part_kv, o)
    sum_feed.send(*o.out.sums)
    o.layer_output = place_rows(o.meta, o.out.parts, n, m, BF)
    o.pin(sum_kv)

    red_kv_out = sum_kv.finish(part_kv, o)
    o.red_outward = red_kv_out[2 * PRE_DEV :]
    d_prefix = red_kv_out[: 2 * PRE_DEV].astype(BF).reshape(2, PRE_DEV, width)
    d_parts = lax.dynamic_update_slice(o.out.d_parts, d_prefix, (1, 0, 0))
    o.d_projected = jnp.concatenate([d_parts[0], d_parts[1], d_parts[2]], axis=1)
    o.out.d_send

    def part_inward(b):
        return jnp.einsum(
            "td,tn->dn", column_block(o.normed_one, b), o.d_projected, preferred_element_type=FP
        )

    o.far = part_inward(ring.half)
    o.pin()
    sum_inward = ring.scatter(o.out.far)
    o.kept, o.away = rows_matmul(
        o.meta, "in_back", o.d_projected, in_blocks, m, True, (0, 3 * share), "three"
    )
    o.pin(sum_inward)
    kept, got = o.out.kept, team.cross(o.out.away)
    sum_inward.advance(part_inward, o)
    o.kept, o.got = kept, got
    o.pin()
    kept, got = o.out.kept, o.out.got
    arrived = team.send_sums(kept, got)
    o.pin(sum_inward)
    sum_inward.advance(part_inward, o)
    o.terms = [kept, got] + arrived
    o.pin()
    o.own, o.gain_one = first_norm_back(
        o.meta, o.out.terms, o.source, o.d_hidden, gains, n
    )
    o.pin()
    parts = team.send_own(o.out.own)
    o.pin(sum_inward)
    sum_inward.advance(part_inward, o)
    o.parts = parts
    o.pin(sum_feed)
    o.parts = team.send_half(o.parts)
    o.red_feed = sum_feed.finish(o)
    o.out.both
    gain_parts = jnp.concatenate([o.out.gain_one, o.out.gain_two], axis=0).reshape(2, n, share)
    o.gain_parts = jnp.take(gain_parts, blocks_of, axis=1).reshape(2, model)
    red_feed, red_outward = o.out.red_feed, o.out.red_outward
    o.squares = jnp.sum(red_outward * red_outward) + jnp.sum(red_feed * red_feed)
    o.pin()
    o.input_grad = place_rows(o.meta, o.out.parts, n, m, FP)
    o.pin(sum_inward)
    red_inward = sum_inward.finish(part_inward, o)
    layer_output, input_grad, gain_parts = o.out.layer_output, o.out.input_grad, o.out.gain_parts

    squares = jnp.sum(red_inward * red_inward) + o.out.squares
    sums = jnp.concatenate([gain_parts, jnp.full((1, model), squares, FP)], axis=0)
    sums = total_of_all(sums, n, m)
    gain_sums = sums[:2]
    grad_norm = jnp.sqrt(sums[2, 0] + jnp.sum(gain_sums * gain_sums))
    factor = CLIP_NORM / jnp.maximum(grad_norm, CLIP_NORM)
    red_gains = lax.dynamic_slice(gain_sums, (0, device * share), (2, share))

    new = update_matrices(
        jnp.reshape(factor, (1,)),
        (
            (
                red_inward, flat_inward(inward), flat_inward(moment_inward),
                flat_inward(variance_inward), flat_inward(average_inward),
            ),
            (red_outward, outward, moment_outward, variance_outward, average_outward),
            (red_feed, expand, moment_expand, variance_expand, average_expand),
            (red_feed, contract, moment_contract, variance_contract, average_contract),
        ),
        (RATE_INWARD, RATE_OUTWARD, RATE_EXPAND, RATE_CONTRACT),
        4,
    )
    in_new = tuple(jnp.transpose(array, (1, 0, 2)) for array in new[:4])
    gain_new = adamw(
        norm_gains, red_gains * factor, moment_gains, variance_gains, average_gains, RATE_GAINS, 0.0
    )
    return (
        (layer_output, input_grad, jnp.reshape(grad_norm, (1,)))
        + in_new + tuple(new[4:]) + gain_new
    )


def solution(mesh):
    in_place = P("seq", None, "head")
    out_place = P("head", "seq")
    up_place = P("seq", "head")
    gain_place = P(None, "seq")
    weights = (in_place, out_place, up_place, out_place, gain_place)
    placed = (P("seq", None), P("seq", None), P(), P("seq")) + weights * 4
    results = (P("seq", None), P("seq", None), P())
    for place in weights:
        results += (place,) * 4
    return jax.shard_map(
        functools.partial(local, mesh.shape["seq"], mesh.shape["head"]),
        mesh=mesh,
        in_specs=placed,
        out_specs=results,
        check_vma=False,
    )
```
